256 devices in a mesh: dp: 8 (over z), group: 4 (over x), tensor: 8 (over y, core).
Axes of the slice: x: 4, y: 4, z: 8, core: 2. Of those that a mesh axis runs over, the one named last changes fastest.
Arguments:
- learn_x: bfloat16 [32768, 8192], P(('dp', 'group'), 'tensor'), may hold values from -6.5 to 6.5
- learn_dy: bfloat16 [32768, 1024], P(('dp', 'group'), 'tensor'), may hold values from -0.59765625 to 0.59765625
- block_tenant: int32 [256], P(('dp', 'group')), may hold values from 0 to 63, as said below
- block_count: int32 [256], P(('dp', 'group')), may hold values from 32 to 128
- adapter_a: float32 [64, 32, 8192], P(('dp', 'group'), None, 'tensor'), may hold values from -0.0625 to 0.0625
- adapter_b: float32 [64, 32, 1024], P(('dp', 'group'), None, 'tensor'), may hold values from -0.1875 to 0.1875
- moment_a: float32 [64, 32, 8192], P(('dp', 'group'), None, 'tensor'), may hold values from -12 to 12
- moment_b: float32 [64, 32, 1024], P(('dp', 'group'), None, 'tensor'), may hold values from -12 to 12
- second_a: float32 [64, 32, 8192], P(('dp', 'group'), None, 'tensor'), may hold values from 0.01 to 0.5
- second_b: float32 [64, 32, 1024], P(('dp', 'group'), None, 'tensor'), may hold values from 0.01 to 0.5
- tenant_group: int32 [64], replicated, may hold values from 0 to 3, as said below
- decode_inputs: bfloat16 [4, 1024, 2, 8192], P('group', 'dp'), may hold values from -6.5 to 6.5
- dec_weight: bfloat16 [8192, 1024], P(None, 'tensor'), may hold values from -0.0625 to 0.0625
- request_adapter: int32 [4, 1024], P('group', 'dp'), may hold values from 0 to 63, as said below
Outputs:
- updated_a: float32 [64, 32, 8192], P(('dp', 'group'), None, 'tensor')
- updated_b: float32 [64, 32, 1024], P(('dp', 'group'), None, 'tensor')
- moment_a_new: float32 [64, 32, 8192], P(('dp', 'group'), None, 'tensor')
- moment_b_new: float32 [64, 32, 1024], P(('dp', 'group'), None, 'tensor')
- second_a_new: float32 [64, 32, 8192], P(('dp', 'group'), None, 'tensor')
- second_b_new: float32 [64, 32, 1024], P(('dp', 'group'), None, 'tensor')
- decode_output: bfloat16 [4, 1024, 2, 1024], P('group', 'dp', None, 'tensor')
The draws below stay inside these ranges and needn't reach their ends.
Inputs may be any that keep to these rules, and one draw needn't show every extreme that they name: `block_tenant`: the state of tenant t lies on index t // 2 of dp+group, whose group index is (t // 2) % 4. The 8 blocks of one device (one index of dp+group) name tenants of each group index exactly 8 / 4 times, in any order. `tenant_group`: for each index i of dp, the tenants i * 8 to (i + 1) * 8 - 1 include exactly 2 tenants of each group; so each group serves exactly 16 tenants. Each request's tenant is served by the request's group: tenant_group[request_adapter[g, q]] == g; every tenant that a group serves is named by some request of that group.
All inputs are finite; a program needn't handle non-finite values.
Results may differ from the reference program's by a relative error of at most 0.012.
Values may be sent and summed in bfloat16 or wider, within the bound.
No kernel may reach another device: no remote copies, remote signals or barrier semaphores. Data moves between devices by JAX's collectives and lax.ppermute only.
A program may use at most 64 MiB of HBM per device.

```python
import math
import jax
import jax.numpy as jnp
from jax import lax

MODEL_WIDTH = 8192
VALUE_OUTPUTS = 1024
R = 32
TENANTS = 64
BLK = 128
NBLK = 8
DECODE_STEPS = 2
STEP_NUM = 10
TEN_DEV = 2
SPAN = 8
SERVED = 16
BLOCKS = 256
TOKENS = 32768
REQS = 1024
N_DP = 8
N_GROUP = 4


def assign_groups(key):
    span_length = N_GROUP * TEN_DEV
    row_keys = jax.random.split(jax.random.fold_in(key, 11), N_DP)
    orders = jax.vmap(lambda one_key: jax.random.permutation(one_key, span_length))(row_keys)
    return (orders // TEN_DEV).reshape(TENANTS).astype(jnp.int32)


def channel_offset(key):
    offset_key = jax.random.fold_in(key, 101)
    return 0.5 * jax.random.truncated_normal(offset_key, -3.0, 3.0, (MODEL_WIDTH,), jnp.float32)


def draw_learn_x(key, part):
    offset = channel_offset(key)
    key = jax.random.fold_in(key, 13)
    noise_key = jax.random.fold_in(key, 0)
    noise = jax.random.truncated_normal(noise_key, -5.0, 5.0, (TOKENS, MODEL_WIDTH), jnp.float32)
    return (offset[None, :] + noise).astype(jnp.bfloat16)


def draw_decode_inputs(key, part):
    offset = channel_offset(key)
    key = jax.random.fold_in(key, 17)
    noise_key = jax.random.fold_in(key, 0)
    noise = jax.random.truncated_normal(noise_key, -5.0, 5.0, (N_GROUP, REQS, DECODE_STEPS, MODEL_WIDTH), jnp.float32)
    return (offset + noise).astype(jnp.bfloat16)


def draw_block_tenant(key, part):
    key = jax.random.fold_in(key, 7)
    order_key, row_key, slot_key = jax.random.split(key, 3)
    device_total = N_DP * N_GROUP
    orders = jax.vmap(lambda one_key: jax.random.permutation(one_key, NBLK))(jax.random.split(order_key, device_total))
    flat_orders = orders.reshape(-1).astype(jnp.int32)
    columns = flat_orders % N_GROUP
    rows = jax.random.randint(row_key, (BLOCKS,), 0, N_DP).astype(jnp.int32)
    slots = jax.random.randint(slot_key, (BLOCKS,), 0, TEN_DEV).astype(jnp.int32)
    device_of = jnp.arange(BLOCKS, dtype=jnp.int32) // NBLK
    low_spot = (device_of == 0) & (flat_orders == 0)
    high_spot = (device_of == device_total - 1) & (flat_orders == N_GROUP - 1)
    rows = jnp.where(low_spot, 0, jnp.where(high_spot, N_DP - 1, rows))
    slots = jnp.where(low_spot, 0, jnp.where(high_spot, TEN_DEV - 1, slots))
    return (rows * SPAN + columns * TEN_DEV + slots).astype(jnp.int32)


def draw_tenant_group(key, part):
    mapping = assign_groups(key)
    return mapping


def draw_request_adapter(key, part):
    mapping = assign_groups(key)
    key = jax.random.fold_in(key, 5)
    first_key, second_key = jax.random.split(key)
    group_ids = jnp.arange(N_GROUP, dtype=jnp.int32)[:, None]
    outside = (mapping[None, :] != group_ids).astype(jnp.int32)
    served_ids = jnp.argsort(outside, axis=1, stable=True)[:, :SERVED]
    chosen = jax.random.randint(first_key, (N_GROUP, REQS), 0, SERVED)
    spots = jax.vmap(lambda one_key: jax.random.permutation(one_key, REQS))(jax.random.split(second_key, N_GROUP))
    chosen = jnp.where(spots < SERVED, spots, chosen)
    return jnp.take_along_axis(served_ids, chosen, axis=1).astype(jnp.int32)


def set_ends(entries, rng, low, high):
    longest = entries.shape.index(max(entries.shape))
    spots = []
    for shift in (0, 1):
        where = [jax.random.randint(jax.random.fold_in(rng, axis), (), 0, length) for axis, length in enumerate(entries.shape)]
        where[longest] = (where[longest] + shift) % entries.shape[longest]
        spots.append(tuple(where))
    return entries.at[spots[0]].set(low).at[spots[1]].set(high)


def level_of(stream_key, extent, pieces, least, high):
    def one(axis_at, shards_of):
        steps = jax.random.uniform(jax.random.fold_in(jax.random.fold_in(stream_key, 6), axis_at), (shards_of,), jnp.float32, least / len(pieces), high / len(pieces))
        return jnp.repeat(jnp.exp(steps), extent[axis_at] // shards_of).reshape((-1,) + (1,) * (len(extent) - axis_at - 1))

    loudness = one(*pieces[0])
    for cut in pieces[1:]:
        loudness = loudness * one(*cut)
    return loudness


def scatter_about(own_key, shape, scale, bound, cuts=(), kind=jnp.bfloat16):
    array = scale * jax.random.normal(own_key, shape, jnp.float32)
    if cuts:
        array = array * level_of(own_key, shape, cuts, -0.22, 0.18)
    return jnp.clip(array, -bound, bound).astype(kind)


def setup_inputs(seed: int = 0) -> dict:
    key_of = jax.random.split(jax.random.key(seed), 15)
    return {
        "learn_x": draw_learn_x(jax.random.fold_in(key_of[14], 71), 0),
        "learn_dy": scatter_about(key_of[1], (TOKENS, VALUE_OUTPUTS), 0.1, 0.59765625, ((0, 32), (1, 8))),
        "block_tenant": draw_block_tenant(jax.random.fold_in(key_of[14], 71), 0),
        "block_count": set_ends(jax.random.randint(key_of[3], (BLOCKS,), BLK // 4, BLK + 1), jax.random.fold_in(key_of[3], 1), BLK // 4, BLK).astype(jnp.int32),
        "adapter_a": scatter_about(key_of[4], (TENANTS, R, MODEL_WIDTH), MODEL_WIDTH ** -0.5, 0.0625, ((0, 32), (2, 8)), jnp.float32),
        "adapter_b": scatter_about(key_of[5], (TENANTS, R, VALUE_OUTPUTS), VALUE_OUTPUTS ** -0.5, 0.1875, ((0, 32), (2, 8)), jnp.float32),
        "moment_a": scatter_about(key_of[6], (TENANTS, R, MODEL_WIDTH), 2.0, 12.0, ((0, 32), (2, 8)), jnp.float32),
        "moment_b": scatter_about(key_of[7], (TENANTS, R, VALUE_OUTPUTS), 2.0, 12.0, ((0, 32), (2, 8)), jnp.float32),
        "second_a": jnp.clip(jnp.exp(math.log(0.5) - 3.912023 * jax.random.uniform(key_of[8], (TENANTS, R, MODEL_WIDTH), jnp.float32) ** level_of(key_of[8], (TENANTS, R, MODEL_WIDTH), ((0, 32), (2, 8)), -0.2, 0.2)), 0.01, 0.5),
        "second_b": jnp.clip(jnp.exp(math.log(0.5) - 3.912023 * jax.random.uniform(key_of[9], (TENANTS, R, VALUE_OUTPUTS), jnp.float32) ** level_of(key_of[9], (TENANTS, R, VALUE_OUTPUTS), ((0, 32), (2, 8)), -0.2, 0.2)), 0.01, 0.5),
        "tenant_group": draw_tenant_group(jax.random.fold_in(key_of[14], 71), 0),
        "decode_inputs": draw_decode_inputs(jax.random.fold_in(key_of[14], 71), 0),
        "dec_weight": scatter_about(key_of[12], (MODEL_WIDTH, VALUE_OUTPUTS), MODEL_WIDTH ** -0.5, 0.0625, ((1, 8),)),
        "request_adapter": draw_request_adapter(jax.random.fold_in(key_of[14], 71), 0),
    }


adapter_scale = 2.0
beta_one = 0.9
beta_two = 0.999
step_rate = 0.001
adam_eps = 1e-08

def adam_update(weights, moment, second, gradient):
    moment_new = beta_one * moment + (1.0 - beta_one) * gradient
    second_new = beta_two * second + (1.0 - beta_two) * gradient * gradient
    unbiased_m = moment_new / (1.0 - beta_one ** STEP_NUM)
    unbiased_v = second_new / (1.0 - beta_two ** STEP_NUM)
    weights_new = weights - step_rate * unbiased_m / (jnp.sqrt(unbiased_v) + adam_eps)
    return (weights_new, moment_new, second_new)

def reference(learn_x, learn_dy, block_tenant, block_count, adapter_a, adapter_b, moment_a, moment_b, second_a, second_b, tenant_group, decode_inputs, dec_weight, request_adapter):
    block_total = block_tenant.shape[0]
    input_blocks = learn_x.reshape(block_total, BLK, MODEL_WIDTH)
    alive_rows = (jnp.arange(BLK, dtype=jnp.int32)[None, :] < block_count[:, None]).astype(jnp.bfloat16)
    cotan_blocks = learn_dy.reshape(block_total, BLK, VALUE_OUTPUTS) * alive_rows[:, :, None]
    a_half = adapter_a.astype(jnp.bfloat16)
    b_half = adapter_b.astype(jnp.bfloat16)

    def accumulate(totals, element):
        grad_a, grad_b = totals
        input_block, output_gradient_block, tenant = element
        a_tenant = a_half[tenant]
        b_tenant = b_half[tenant]
        low_rank_input = jnp.dot(input_block, a_tenant.T, preferred_element_type=jnp.float32).astype(jnp.bfloat16)
        low_rank_backward = jnp.dot(output_gradient_block, b_tenant.T, preferred_element_type=jnp.float32).astype(jnp.bfloat16)
        down_term = adapter_scale * jnp.dot(low_rank_backward.T, input_block, preferred_element_type=jnp.float32)
        up_term = adapter_scale * jnp.dot(low_rank_input.T, output_gradient_block, preferred_element_type=jnp.float32)
        return ((grad_a.at[tenant].add(down_term), grad_b.at[tenant].add(up_term)), None)
    start_totals = (jnp.zeros((TENANTS, R, MODEL_WIDTH), jnp.float32), jnp.zeros((TENANTS, R, VALUE_OUTPUTS), jnp.float32))
    (grad_a, grad_b), _ = lax.scan(accumulate, start_totals, (input_blocks, cotan_blocks, block_tenant))
    updated_a, moment_a_new, second_a_new = adam_update(adapter_a, moment_a, second_a, grad_a)
    updated_b, moment_b_new, second_b_new = adam_update(adapter_b, moment_b, second_b, grad_b)
    fresh_a = updated_a.astype(jnp.bfloat16)
    fresh_b = updated_b.astype(jnp.bfloat16)
    group_count = decode_inputs.shape[0]
    request_total = decode_inputs.shape[1]
    flat_x = decode_inputs.reshape(-1, MODEL_WIDTH)
    frozen_output = jnp.dot(flat_x, dec_weight, preferred_element_type=jnp.float32)
    frozen_output = frozen_output.reshape(group_count, request_total, DECODE_STEPS, VALUE_OUTPUTS)

    def request_adapter_delta(element):
        x_request, tenant = element
        decode_input = jnp.dot(x_request, fresh_a[tenant].T, preferred_element_type=jnp.float32).astype(jnp.bfloat16)
        return jnp.dot(decode_input, fresh_b[tenant], preferred_element_type=jnp.float32)
    adapter_delta = lax.map(request_adapter_delta, (decode_inputs.reshape(-1, DECODE_STEPS, MODEL_WIDTH), request_adapter.reshape(-1)))
    adapter_delta = adapter_delta.reshape(group_count, request_total, DECODE_STEPS, VALUE_OUTPUTS)
    served_mask = (tenant_group[request_adapter] == jnp.arange(group_count, dtype=jnp.int32)[:, None]).astype(jnp.float32)
    adapter_delta = adapter_delta * served_mask[:, :, None, None]
    decode_output = (frozen_output + adapter_scale * adapter_delta).astype(jnp.bfloat16)
    return (updated_a, updated_b, moment_a_new, moment_b_new, second_a_new, second_b_new, decode_output)
```

```python
import functools

import jax
import jax.numpy as jnp
from jax import lax
from jax.experimental import pallas as pl
from jax.experimental.pallas import tpu as pltpu
from jax.sharding import PartitionSpec as P

STEP_NUM = 10

adapter_scale = 2.0
beta_one = 0.9
beta_two = 0.999
step_rate = 0.001
adam_eps = 1e-08

BF = jnp.bfloat16
F32 = jnp.float32
VMEM_LIMIT = 40 * 1024 * 1024


def dot(a, b, dims):
    return lax.dot_general(a, b, (dims, ((), ())), preferred_element_type=F32)


def shift(x, axis, distance):
    size = lax.axis_size(axis)
    return lax.ppermute(x, axis, [(i, (i + distance) % size) for i in range(size)])


def spread(x, axis):
    return [x] + [shift(x, axis, d) for d in range(1, lax.axis_size(axis))]


def vmem(n):
    return [pl.BlockSpec(memory_space=pltpu.VMEM)] * n


def smem(n):
    return [pl.BlockSpec(memory_space=pltpu.SMEM)] * n


PARAMS = pltpu.CompilerParams(vmem_limit_bytes=VMEM_LIMIT)


def pack_kernel(source, count, x_ref, dy_ref, *outs):
    step = pl.program_id(0)
    rows, width = x_ref.shape
    live = lax.broadcasted_iota(jnp.int32, dy_ref.shape, 0) < count[source[step]]
    dy = jnp.where(live, dy_ref[...].astype(F32), 0.0).astype(BF)
    for d, out in enumerate(outs):

        @pl.when(step // 2 == d)
        def _():
            out[:, :width] = x_ref[...]
            out[:, width:] = dy


def pack(source, count, learn_x, learn_dy, groups):
    blocks = source.shape[0]
    rows = learn_x.shape[0] // blocks
    width, width_b = learn_x.shape[1], learn_dy.shape[1]
    each = blocks // groups
    return pl.pallas_call(
        pack_kernel,
        grid_spec=pltpu.PrefetchScalarGridSpec(
            num_scalar_prefetch=2,
            grid=(blocks,),
            in_specs=[
                pl.BlockSpec((rows, width), lambda s, source, count: (source[s], 0)),
                pl.BlockSpec((rows, width_b), lambda s, source, count: (source[s], 0)),
            ],
            out_specs=[
                pl.BlockSpec(
                    (rows, width + width_b),
                    lambda s, source, count, d=d: (jnp.clip(s - each * d, 0, each - 1), 0),
                )
                for d in range(groups)
            ],
        ),
        out_shape=[jax.ShapeDtypeStruct((each * rows, width + width_b), BF)] * groups,
        compiler_params=PARAMS,
    )(source, count, learn_x, learn_dy)


def low_kernel(rank, rows, index, *refs):
    *refs, out, table = refs
    adapters, blocks = refs[:8], refs[8:]
    wide = blocks[0].shape[1]
    width = wide - 128
    for d, ref in enumerate(adapters):
        for j in range(2):
            table[2 * d + j] = ref[j * rank : (j + 1) * rank, :]
    for s in range(2 * len(blocks)):
        ref = blocks[s // 2]
        part = pl.ds((s % 2) * rows, rows)
        chosen = table[index[s]]
        low_in = dot(chosen[:, :width], ref[part, :width], ((1,), (1,)))
        low_back = dot(chosen[:, width:], ref[part, width:], ((1,), (1,)))
        out[s * 2 * rank : s * 2 * rank + rank, :] = low_in.astype(BF)
        out[s * 2 * rank + rank : (s + 1) * 2 * rank, :] = low_back.astype(BF)


def low(index, adapters, blocks, rank):
    rows = blocks[0].shape[0] // 2
    wide = blocks[0].shape[1]
    return pl.pallas_call(
        functools.partial(low_kernel, rank, rows),
        in_specs=smem(1) + vmem(len(adapters) + len(blocks)),
        out_specs=pl.BlockSpec(memory_space=pltpu.VMEM),
        out_shape=jax.ShapeDtypeStruct((2 * len(blocks) * 2 * rank, rows), BF),
        scratch_shapes=[pltpu.VMEM((2 * len(adapters), rank, wide), BF)],
        compiler_params=PARAMS,
    )(index, *adapters, *blocks)


def grad_kernel(rank, rows, parts, groups, index, *refs):
    lows, blocks = refs[:parts], refs[parts : parts + groups]
    outs, sums = refs[parts + groups : -1], refs[-1]
    wide = blocks[0].shape[1]
    width = wide - 128
    total = lows[0][...].astype(F32)
    for ref in lows[1:]:
        total = total + ref[...].astype(F32)
    total = total.astype(BF)
    sums[...] = jnp.zeros_like(sums)
    for s in range(2 * groups):
        ref = blocks[s // 2]
        part = pl.ds((s % 2) * rows, rows)
        low_in = total[s * 2 * rank : s * 2 * rank + rank]
        low_back = total[s * 2 * rank + rank : (s + 1) * 2 * rank]
        here = index[s]
        sums[here, :, :width] += dot(low_back, ref[part, :width], ((1,), (0,)))
        sums[here, :, width:] += dot(low_in, ref[part, width:], ((1,), (0,)))
    for d, out in enumerate(outs):
        for j in range(2):
            out[j * rank : (j + 1) * rank, :] = (adapter_scale * sums[2 * d + j]).astype(BF)


def grad(index, lows, blocks, rank, targets):
    rows = blocks[0].shape[0] // 2
    wide = blocks[0].shape[1]
    return pl.pallas_call(
        functools.partial(grad_kernel, rank, rows, len(lows), len(blocks)),
        in_specs=smem(1) + vmem(len(lows) + len(blocks)),
        out_specs=vmem(targets),
        out_shape=[jax.ShapeDtypeStruct((2 * rank, wide), BF)] * targets,
        scratch_shapes=[pltpu.VMEM((2 * targets, rank, wide), F32)],
        compiler_params=PARAMS,
    )(index, *lows, *blocks)


def adam_update(weights, moment, second, gradient):
    moment_new = beta_one * moment + (1.0 - beta_one) * gradient
    second_new = beta_two * second + (1.0 - beta_two) * gradient * gradient
    unbiased_m = moment_new / (1.0 - beta_one**STEP_NUM)
    unbiased_v = second_new / (1.0 - beta_two**STEP_NUM)
    weights_new = weights - step_rate * unbiased_m / (jnp.sqrt(unbiased_v) + adam_eps)
    return (weights_new, moment_new, second_new)


def adam_kernel(parts, *refs):
    grads, refs = refs[:parts], refs[parts:]
    state_a, state_b = refs[0:3], refs[3:6]
    new_a, new_b, fresh = refs[6:9], refs[9:12], refs[12]
    width = state_a[0].shape[1]
    total = grads[0][...].astype(F32)
    for ref in grads[1:]:
        total = total + ref[...].astype(F32)
    for state, new, cols in (
        (state_a, new_a, slice(0, width)),
        (state_b, new_b, slice(width, None)),
    ):
        values = adam_update(*[ref[...] for ref in state], total[:, cols])
        for ref, value in zip(new, values):
            ref[...] = value
        fresh[:, cols] = values[0].astype(BF)


def adam(grads, state_a, state_b):
    rows, width = state_a[0].shape
    width_b = state_b[0].shape[1]
    wide = width + width_b
    tile = 16
    steps = rows // tile

    def spec(w):
        return pl.BlockSpec((tile, w), lambda i: (i, 0))

    return pl.pallas_call(
        functools.partial(adam_kernel, len(grads)),
        grid=(steps,),
        in_specs=[spec(wide)] * len(grads) + [spec(width)] * 3 + [spec(width_b)] * 3,
        out_specs=[spec(width)] * 3 + [spec(width_b)] * 3 + [spec(wide)],
        out_shape=[jax.ShapeDtypeStruct((rows, width), F32)] * 3
        + [jax.ShapeDtypeStruct((rows, width_b), F32)] * 3
        + [jax.ShapeDtypeStruct((rows, wide), BF)],
        compiler_params=PARAMS,
    )(*grads, *state_a, *state_b)


def pick_kernel(rank, index, *refs):
    *refs, out = refs
    for i in range(2):
        device, slot = index[i] // 2, index[i] % 2
        for d, ref in enumerate(refs):

            @pl.when(device == d)
            def _():
                out[i * rank : (i + 1) * rank, :] = ref[
                    pl.ds(pl.multiple_of(slot * rank, rank), rank), :
                ]


def pick(index, arrays, rank):
    return pl.pallas_call(
        functools.partial(pick_kernel, rank),
        in_specs=smem(1) + vmem(len(arrays)),
        out_specs=pl.BlockSpec(memory_space=pltpu.VMEM),
        out_shape=jax.ShapeDtypeStruct(arrays[0].shape, BF),
        compiler_params=PARAMS,
    )(index, *arrays)


def decode_in_kernel(rank, slots, x, *refs):
    *refs, out = refs
    width = x.shape[1]
    total = jnp.zeros(out.shape, F32)
    for d, ref in enumerate(refs):
        both = dot(ref[:, :width], x[...], ((1,), (1,)))
        for j in range(2):
            total += jnp.where(slots[...] == 2 * d + j, both[j * rank : (j + 1) * rank], 0.0)
    out[...] = total


def decode_in(slots, x, fresh, rank):
    return pl.pallas_call(
        functools.partial(decode_in_kernel, rank),
        in_specs=vmem(2 + len(fresh)),
        out_specs=pl.BlockSpec(memory_space=pltpu.VMEM),
        out_shape=jax.ShapeDtypeStruct((rank, x.shape[0]), F32),
        compiler_params=PARAMS,
    )(slots, x, *fresh)


def decode_out_kernel(rank, parts, slots, frozen, *refs):
    lows, fresh, out = refs[:parts], refs[parts:-1], refs[-1]
    width_b = frozen.shape[1]
    total = lows[0][...]
    for ref in lows[1:]:
        total = total + ref[...]
    total = total.astype(BF).astype(F32)
    result = jnp.zeros(frozen.shape, F32)
    for d, ref in enumerate(fresh):
        both = jnp.concatenate(
            [jnp.where(slots[...] == 2 * d + j, total, 0.0) for j in range(2)], axis=0
        )
        result += dot(both.T.astype(BF), ref[...], ((1,), (0,)))
    out[...] = (frozen[...] + adapter_scale * result).astype(BF)


def decode_out(slots, frozen, lows, fresh, rank):
    width_b = frozen.shape[1]
    wide = fresh[0].shape[1]
    whole = [pl.BlockSpec(a.shape, lambda i: (0, 0)) for a in (slots, frozen, *lows)]
    ends = [
        pl.BlockSpec((2 * rank, width_b), lambda i: (0, wide // width_b - 1)) for _ in fresh
    ]
    return pl.pallas_call(
        functools.partial(decode_out_kernel, rank, len(lows)),
        grid=(1,),
        in_specs=whole + ends,
        out_specs=pl.BlockSpec(frozen.shape, lambda i: (0, 0)),
        out_shape=jax.ShapeDtypeStruct(frozen.shape, BF),
        compiler_params=PARAMS,
    )(slots, frozen, *lows, *fresh)


def column_of(tenant, groups):
    return (tenant // 2) % groups


def local(
    learn_x,
    learn_dy,
    block_tenant,
    block_count,
    adapter_a,
    adapter_b,
    moment_a,
    moment_b,
    second_a,
    second_b,
    tenant_group,
    decode_inputs,
    dec_weight,
    request_adapter,
):
    groups = lax.axis_size("group")
    rows_dp = lax.axis_size("dp")
    group = lax.axis_index("group")
    row = lax.axis_index("dp")
    owned, rank, width = adapter_a.shape
    width_b = adapter_b.shape[2]
    span = groups * owned

    def flat(x):
        return x.reshape(owned * rank, x.shape[2])

    own = jnp.concatenate([flat(adapter_a), flat(adapter_b)], axis=1).astype(BF)
    table = spread(own, "dp")

    blocks = block_tenant.shape[0]
    column = column_of(block_tenant, groups)
    distance = (column - group) % groups
    earlier = jnp.tril(distance[:, None] == distance[None, :], -1).astype(jnp.int32)
    place = distance * (blocks // groups) + jnp.sum(earlier, axis=1)
    here = place[None, :] == jnp.arange(blocks, dtype=jnp.int32)[:, None]
    source = jnp.sum(
        jnp.where(here, jnp.arange(blocks, dtype=jnp.int32)[None, :], 0), axis=1, dtype=jnp.int32
    )
    packed = pack(source, block_count, learn_x, learn_dy, groups)
    tenants = jnp.sum(jnp.where(here, block_tenant[None, :], 0), axis=1, dtype=jnp.int32)
    tenants = tenants.reshape(groups, blocks // groups)
    arrived = [packed[0]] + [shift(packed[d], "group", d) for d in range(1, groups)]
    tenants = jnp.concatenate(
        [tenants[0]] + [shift(tenants[d], "group", d) for d in range(1, groups)]
    )
    tenant_row, tenant_slot = tenants // span, tenants % owned

    partial = low(((row - tenant_row) % rows_dp) * owned + tenant_slot, table, arrived, rank)
    tensor_size = lax.axis_size("tensor")
    lows = [partial] + [
        lax.ppermute(partial, "tensor", [(i, i ^ d) for i in range(tensor_size)])
        for d in range(1, tensor_size)
    ]
    sums = grad(
        ((tenant_row - row) % rows_dp) * owned + tenant_slot, lows, arrived, rank, rows_dp
    )
    pieces = [sums[0]] + [shift(sums[d], "dp", d) for d in range(1, rows_dp)]
    *new, fresh = adam(
        pieces,
        [flat(x) for x in (adapter_a, moment_a, second_a)],
        [flat(x) for x in (adapter_b, moment_b, second_b)],
    )

    in_row = spread(fresh, "group")
    tenant_ids = jnp.arange(tenant_group.shape[0], dtype=jnp.int32)
    served = (tenant_group == group).astype(jnp.int32)
    by_row = served.reshape(rows_dp, span)
    slot_of = jnp.cumsum(by_row, axis=1) - by_row
    mine = lax.dynamic_slice_in_dim(by_row, row, 1, 0)[0]
    mine_slot = lax.dynamic_slice_in_dim(slot_of, row, 1, 0)[0]
    position = jnp.arange(span, dtype=jnp.int32)
    relative = ((group - position // owned) % groups) * owned + position % owned
    wanted = jnp.sum(
        jnp.where(
            (mine[None, :] == 1)
            & (mine_slot[None, :] == jnp.arange(owned, dtype=jnp.int32)[:, None]),
            relative[None, :],
            0,
        ),
        axis=1,
        dtype=jnp.int32,
    )
    served_fresh = spread(pick(wanted, in_row, rank), "dp")

    slot_here = ((row - tenant_ids // span) % rows_dp) * owned + slot_of.reshape(-1)
    slot_here = jnp.where(served == 1, slot_here, -1)
    request_slot = jnp.sum(
        jnp.where(request_adapter[0][:, None] == tenant_ids[None, :], slot_here[None, :], 0),
        axis=1,
        dtype=jnp.int32,
    )
    requests = decode_inputs[0]
    steps = requests.shape[1]
    count = requests.shape[0] * steps
    slots = jnp.broadcast_to(request_slot[:, None], (requests.shape[0], steps)).reshape(1, count)
    frozen = jnp.einsum("qsd,dk->qsk", requests, dec_weight, preferred_element_type=F32)
    frozen = frozen.reshape(count, width_b)
    x_slice = lax.dynamic_slice_in_dim(requests, lax.axis_index("tensor") * width, width, 2)
    dec_part = decode_in(slots, x_slice.reshape(count, width), served_fresh, rank)
    dec_parts = [dec_part] + [
        lax.ppermute(dec_part, "tensor", [(i, i ^ d) for i in range(tensor_size)])
        for d in range(1, tensor_size)
    ]
    decoded = decode_out(slots, frozen, dec_parts, served_fresh, rank)
    new_a = [x.reshape(adapter_a.shape) for x in new[:3]]
    new_b = [x.reshape(adapter_b.shape) for x in new[3:]]
    return (
        new_a[0],
        new_b[0],
        new_a[1],
        new_b[1],
        new_a[2],
        new_b[2],
        decoded.reshape((1,) + requests.shape[:2] + (width_b,)),
    )


def solution(mesh):
    state = P(("dp", "group"), None, "tensor")
    return jax.shard_map(
        local,
        mesh=mesh,
        in_specs=(
            P(("dp", "group"), "tensor"),
            P(("dp", "group"), "tensor"),
            P(("dp", "group")),
            P(("dp", "group")),
            state,
            state,
            state,
            state,
            state,
            state,
            P(),
            P("group", "dp", None, None),
            P(None, "tensor"),
            P("group", "dp"),
        ),
        out_specs=(
            state,
            state,
            state,
            state,
            state,
            state,
            P("group", "dp", None, "tensor"),
        ),
        check_vma=False,
    )
```

```python
import functools

import jax
import jax.numpy as jnp
from jax import lax
from jax.experimental import pallas as pl
from jax.experimental.pallas import tpu as pltpu
from jax.sharding import PartitionSpec as P

STEP_NUM = 10

adapter_scale = 2.0
beta_one = 0.9
beta_two = 0.999
step_rate = 0.001
adam_eps = 1e-08

BF = jnp.bfloat16
F32 = jnp.float32
MIB = 1024 * 1024


def dot(a, b, dims):
    return lax.dot_general(a, b, (dims, ((), ())), preferred_element_type=F32)


def shift(x, axis, distance):
    size = lax.axis_size(axis)
    return lax.ppermute(x, axis, [(i, (i + distance) % size) for i in range(size)])


def spread(x, axis):
    return [x] + [shift(x, axis, d) for d in range(1, lax.axis_size(axis))]


def ring(x, size, owned, rank):
    ahead = behind = x
    arrays, firsts = [x], [0]
    hops = size // 2
    for hop in range(1, hops + 1):
        if hop == hops:
            ahead, behind = ahead[:rank], behind[rank:]
        ahead, behind = shift(ahead, "dp", 1), shift(behind, "dp", -1)
        arrays += [ahead, behind]
        firsts += [hop * owned, (size - hop) * owned + (1 if hop == hops else 0)]
    return arrays, firsts


def ring_reduce(x, size):
    hops = size // 2
    half = x[hops].shape[0] // 2
    ahead, behind = x[hops][:half], x[hops][half:]
    for hop in range(hops - 1, 0, -1):
        ahead, behind = shift(ahead, "dp", 1), shift(behind, "dp", -1)
        mine, other = x[hop], x[size - hop]
        if hop == hops - 1:
            ahead = jnp.concatenate([add(mine[:half], ahead), mine[half:]])
            behind = jnp.concatenate([other[:half], add(other[half:], behind)])
        else:
            ahead, behind = add(mine, ahead), add(other, behind)
    return [shift(ahead, "dp", 1), shift(behind, "dp", -1)]


def spot(memory, n=1):
    return [pl.BlockSpec(memory_space=memory)] * n


vmem = functools.partial(spot, pltpu.VMEM)
smem = functools.partial(spot, pltpu.SMEM)
anywhere = functools.partial(spot, pl.ANY)
SMALL = pltpu.CompilerParams(vmem_limit_bytes=14 * MIB)
LARGE = pltpu.CompilerParams(vmem_limit_bytes=56 * MIB)


def shape(dims, dtype=BF):
    return jax.ShapeDtypeStruct(dims, dtype)


def block_of(ref, index, rows):
    return ref.at[pl.ds(pl.multiple_of(index * rows, rows), rows), :]


def fetch(refs, rooms, sems):
    copies = [
        pltpu.make_async_copy(ref, room, sems.at[i]) for i, (ref, room) in enumerate(zip(refs, rooms))
    ]
    for copy in copies:
        copy.start()
    return copies


def begin_kernel(rows, groups, tenant, count, x, dy, adapter_a, adapter_b, *refs):
    packs, own, refs = refs[:groups], refs[groups], refs[groups + 1 :]
    source, ids, dy_here, room, a_here, b_here, half, sems, x_sems, out_sems = refs
    blocks = 2 * groups
    width = x.shape[1]
    loads = fetch([dy, adapter_a, adapter_b], [dy_here, a_here, b_here], sems)
    group = lax.axis_index("group")
    names = [tenant[b] for b in range(blocks)]
    far = [lax.rem(lax.rem(name // 2, groups) - group + groups, groups) for name in names]
    for b in range(blocks):
        place = 2 * far[b]
        for e in range(b):
            place += (far[e] == far[b]).astype(jnp.int32)
        source[place] = b
        ids[place] = names[b]
    moves = []
    for s in range(blocks):
        part = pl.ds((s % 2) * rows, rows)
        moves.append(
            pltpu.make_async_copy(
                block_of(x, source[s], rows), room.at[s // 2, part, :width], x_sems.at[s]
            )
        )
        moves[-1].start()
    loads[0].wait()
    for s in range(blocks):
        block = block_of(dy_here, source[s], rows)[...].astype(F32)
        live = lax.broadcasted_iota(jnp.int32, block.shape, 0) < count[source[s]]
        block = jnp.where(live, block, 0.0).astype(BF)
        room[s // 2, (s % 2) * rows : (s % 2 + 1) * rows, width:] = block
    stores = []
    for d in range(groups):
        lane = lax.broadcasted_iota(jnp.int32, (16, dy.shape[1]), 1)
        both = jnp.where(lane == 0, ids[2 * d], ids[2 * d + 1])
        room[d, 2 * rows :, width:] = both.astype(F32).astype(BF)
        room[d, 2 * rows :, :width] = jnp.zeros((16, width), BF)
        moves[2 * d].wait()
        moves[2 * d + 1].wait()
        stores.append(pltpu.make_async_copy(room.at[d], packs[d], out_sems.at[d]))
        stores[-1].start()
    loads[1].wait()
    half[:, :width] = a_here[...].astype(BF)
    loads[2].wait()
    half[:, width:] = b_here[...].astype(BF)
    stores.append(pltpu.make_async_copy(half, own, sems.at[3]))
    stores[-1].start()
    for store in stores:
        store.wait()


def begin(tenant, count, x, dy, adapter_a, adapter_b, groups):
    rows = x.shape[0] // tenant.shape[0]
    wide = x.shape[1] + dy.shape[1]
    outs = pl.pallas_call(
        functools.partial(begin_kernel, rows, groups),
        in_specs=smem(2) + anywhere(4),
        out_specs=anywhere(groups + 1),
        out_shape=[shape((2 * rows + 16, wide))] * groups + [shape((adapter_a.shape[0], wide))],
        scratch_shapes=[
            pltpu.SMEM((2 * groups,), jnp.int32),
            pltpu.SMEM((2 * groups,), jnp.int32),
            pltpu.VMEM(dy.shape, BF),
            pltpu.VMEM((groups, 2 * rows + 16, wide), BF),
            pltpu.VMEM(adapter_a.shape, F32),
            pltpu.VMEM(adapter_b.shape, F32),
            pltpu.VMEM((adapter_a.shape[0], wide), BF),
            pltpu.SemaphoreType.DMA((4,)),
            pltpu.SemaphoreType.DMA((2 * groups,)),
            pltpu.SemaphoreType.DMA((groups,)),
        ],
        compiler_params=LARGE,
    )(tenant, count, x, dy, adapter_a, adapter_b)
    return outs[:-1], outs[-1]


def low_kernel(rank, rows, firsts, index, *refs):
    parts = len(firsts)
    tables, refs = refs[:parts], refs[parts:]
    *blocks, out, table, here, sems = refs
    wide = table.shape[1]
    width = wide - 128
    used = 2 * rows
    rooms = [
        table.at[first * rank : first * rank + ref.shape[0], :] for first, ref in zip(firsts, tables)
    ]
    rooms += [here.at[d] for d in range(len(blocks))]
    copies = fetch([*tables, *[ref.at[:used, :] for ref in blocks]], rooms, sems)
    for copy in copies[:parts]:
        copy.wait()
    half = used // rows * len(blocks) * rank
    for s in range(2 * len(blocks)):
        if s % 2 == 0:
            copies[parts + s // 2].wait()
        block = here[s // 2, (s % 2) * rows : (s % 2 + 1) * rows, :]
        chosen = block_of(table, index[s], rank)[...]
        low_in = dot(chosen[:, :width], block[:, :width], ((1,), (1,)))
        low_back = dot(chosen[:, width:], block[:, width:], ((1,), (1,)))
        out[s * rank : (s + 1) * rank, :] = low_in.astype(BF)
        out[half + s * rank : half + (s + 1) * rank, :] = low_back.astype(BF)


def low(index, tables, firsts, blocks, rank, rows):
    wide = blocks[0].shape[1]
    total = sum(table.shape[0] for table in tables)
    return pl.pallas_call(
        functools.partial(low_kernel, rank, rows, firsts),
        in_specs=smem() + anywhere(len(tables) + len(blocks)),
        out_specs=vmem()[0],
        out_shape=shape((4 * len(blocks) * rank, rows)),
        scratch_shapes=[
            pltpu.VMEM((total, wide), BF),
            pltpu.VMEM((len(blocks), 2 * rows, wide), BF),
            pltpu.SemaphoreType.DMA((len(tables) + len(blocks),)),
        ],
        compiler_params=LARGE,
    )(index, *tables, *blocks)


def added(refs):
    total = refs[0][...].astype(F32)
    for ref in refs[1:]:
        total = total + ref[...].astype(F32)
    return total


def grad_kernel(rank, rows, parts, index, *refs):
    lows, refs = refs[:parts], refs[parts:]
    groups = lows[0].shape[0] // (4 * rank)
    blocks, refs = refs[:groups], refs[groups:]
    *outs, sums, here, half, sems, out_sems = refs
    width = sums.shape[2] - 128
    copies = fetch(
        [ref.at[: 2 * rows, :] for ref in blocks], [here.at[d] for d in range(groups)], sems
    )
    total = added(lows).astype(BF)
    sums[...] = jnp.zeros_like(sums)
    middle = 2 * groups * rank
    for s in range(2 * groups):
        if s % 2 == 0:
            copies[s // 2].wait()
        block = here[s // 2, (s % 2) * rows : (s % 2 + 1) * rows, :]
        low_in = total[s * rank : (s + 1) * rank]
        low_back = total[middle + s * rank : middle + (s + 1) * rank]
        sums[index[s], :, :width] += dot(low_back, block[:, :width], ((1,), (0,)))
        sums[index[s], :, width:] += dot(low_in, block[:, width:], ((1,), (0,)))
    stores = []
    for d, out in enumerate(outs):
        for j in range(2):
            half[d, j * rank : (j + 1) * rank, :] = (adapter_scale * sums[2 * d + j]).astype(BF)
        stores.append(pltpu.make_async_copy(half.at[d], out, out_sems.at[d]))
        stores[-1].start()
    for store in stores:
        store.wait()


def grad(index, lows, blocks, rank, rows, targets):
    wide = blocks[0].shape[1]
    return pl.pallas_call(
        functools.partial(grad_kernel, rank, rows, len(lows)),
        in_specs=smem() + vmem(len(lows)) + anywhere(len(blocks)),
        out_specs=anywhere(targets),
        out_shape=[shape((2 * rank, wide))] * targets,
        scratch_shapes=[
            pltpu.VMEM((2 * targets, rank, wide), F32),
            pltpu.VMEM((len(blocks), 2 * rows, wide), BF),
            pltpu.VMEM((targets, 2 * rank, wide), BF),
            pltpu.SemaphoreType.DMA((len(blocks),)),
            pltpu.SemaphoreType.DMA((targets,)),
        ],
        compiler_params=LARGE,
    )(index, *lows, *blocks)


def adam_update(weights, moment, second, gradient):
    moment_new = beta_one * moment + (1.0 - beta_one) * gradient
    second_new = beta_two * second + (1.0 - beta_two) * gradient * gradient
    unbiased_m = moment_new / (1.0 - beta_one**STEP_NUM)
    unbiased_v = second_new / (1.0 - beta_two**STEP_NUM)
    weights_new = weights - step_rate * unbiased_m / (jnp.sqrt(unbiased_v) + adam_eps)
    return (weights_new, moment_new, second_new)


def adam_kernel(parts, *refs):
    grads, refs = refs[:parts], refs[parts:]
    states, outs, refs = refs[:6], refs[6:13], refs[13:]
    here, olds, news, fresh, sems, out_sems = refs[0], refs[1:7], refs[7:13], *refs[13:]
    copies = fetch([*states, *grads], [*olds, *[here.at[d] for d in range(parts)]], sems)
    width = olds[0].shape[1]
    for copy in copies:
        copy.wait()
    total = added([here.at[d] for d in range(parts)])
    for first, cols in ((0, slice(0, width)), (3, slice(width, None))):
        values = adam_update(*[ref[...] for ref in olds[first : first + 3]], total[:, cols])
        for ref, value in zip(news[first : first + 3], values):
            ref[...] = value
        fresh[:, cols] = values[0].astype(BF)
    for store in fetch([*news, fresh], outs, out_sems):
        store.wait()


def adam(grads, state_a, state_b):
    rows, width = state_a[0].shape
    width_b = state_b[0].shape[1]
    wide = width + width_b
    states = [pltpu.VMEM((rows, width), F32)] * 3 + [pltpu.VMEM((rows, width_b), F32)] * 3
    return pl.pallas_call(
        functools.partial(adam_kernel, len(grads)),
        in_specs=anywhere(len(grads) + 6),
        out_specs=anywhere(7),
        out_shape=[shape((rows, width), F32)] * 3
        + [shape((rows, width_b), F32)] * 3
        + [shape((rows, wide))],
        scratch_shapes=[pltpu.VMEM((len(grads), rows, wide), BF)]
        + states
        + states
        + [
            pltpu.VMEM((rows, wide), BF),
            pltpu.SemaphoreType.DMA((len(grads) + 6,)),
            pltpu.SemaphoreType.DMA((7,)),
        ],
        compiler_params=LARGE,
    )(*grads, *state_a, *state_b)


def pick_kernel(rank, index, *refs):
    *refs, out = refs
    for i in range(2):
        device, slot = index[i] // 2, index[i] % 2
        for d, ref in enumerate(refs):

            @pl.when(device == d)
            def _():
                out[i * rank : (i + 1) * rank, :] = block_of(ref, slot, rank)[...]


def pick(index, arrays, rank):
    return pl.pallas_call(
        functools.partial(pick_kernel, rank),
        in_specs=smem(1) + vmem(len(arrays)),
        out_specs=vmem()[0],
        out_shape=shape(arrays[0].shape),
        compiler_params=SMALL,
    )(index, *arrays)


def decode_in_kernel(rank, firsts, slots, x, *refs):
    *refs, out = refs
    width = x.shape[1]
    total = jnp.zeros(out.shape, F32)
    for first, ref in zip(firsts, refs):
        both = dot(ref[:, :width], x[...], ((1,), (1,)))
        for j in range(ref.shape[0] // rank):
            total += jnp.where(slots[...] == first + j, both[j * rank : (j + 1) * rank], 0.0)
    out[...] = total


def decode_in(slots, x, fresh, firsts, rank):
    return pl.pallas_call(
        functools.partial(decode_in_kernel, rank, firsts),
        in_specs=vmem(2 + len(fresh)),
        out_specs=vmem()[0],
        out_shape=shape((rank, x.shape[0]), F32),
        compiler_params=SMALL,
    )(slots, x, *fresh)


def decode_out_kernel(rank, parts, firsts, slots, frozen, *refs):
    lows, fresh, out = refs[:parts], refs[parts:-1], refs[-1]
    width_b = frozen.shape[1]
    total = added(lows).astype(BF).astype(F32)
    result = jnp.zeros(frozen.shape, F32)
    for first, ref in zip(firsts, fresh):
        wide = ref.shape[1]
        both = jnp.concatenate(
            [jnp.where(slots[...] == first + j, total, 0.0) for j in range(ref.shape[0] // rank)],
            axis=0,
        )
        result += dot(both.T.astype(BF), ref[:, wide - width_b :], ((1,), (0,)))
    out[...] = (frozen[...] + adapter_scale * result).astype(BF)


def decode_out(slots, frozen, lows, fresh, firsts, rank):
    return pl.pallas_call(
        functools.partial(decode_out_kernel, rank, len(lows), firsts),
        in_specs=vmem(2 + len(lows) + len(fresh)),
        out_specs=vmem()[0],
        out_shape=shape(frozen.shape),
        compiler_params=SMALL,
    )(slots, frozen, *lows, *fresh)


def add(x, y):
    return (x.astype(F32) + y.astype(F32)).astype(x.dtype)


def tensor_parts(x):
    size = lax.axis_size("tensor")
    x = add(x, lax.ppermute(x, "tensor", [(i, i ^ 1) for i in range(size)]))
    return [x] + [
        lax.ppermute(x, "tensor", [(i, (i + 2 * d) % size) for i in range(size)])
        for d in range(1, size // 2)
    ]


def local(
    learn_x,
    learn_dy,
    block_tenant,
    block_count,
    adapter_a,
    adapter_b,
    moment_a,
    moment_b,
    second_a,
    second_b,
    tenant_group,
    decode_inputs,
    dec_weight,
    request_adapter,
):
    groups = lax.axis_size("group")
    rows_dp = lax.axis_size("dp")
    group = lax.axis_index("group")
    row = lax.axis_index("dp")
    owned, rank, width = adapter_a.shape
    width_b = adapter_b.shape[2]
    span = groups * owned
    barrier = lax.optimization_barrier

    def flat(x):
        return x.reshape(owned * rank, x.shape[2])

    blocks = block_tenant.shape[0]
    rows = learn_x.shape[0] // blocks
    each = blocks // groups
    packed, own = begin(
        block_tenant, block_count, learn_x, learn_dy, flat(adapter_a), flat(adapter_b), groups
    )
    arrived = [packed[0]] + [shift(packed[d], "group", d) for d in range(1, groups)]
    tables, firsts = ring(own, rows_dp, owned, rank)
    requests = decode_inputs[0]
    steps = requests.shape[1]
    parts = rows_dp // 2
    part = requests.shape[0] // parts
    tables, requests = barrier((tables, requests))
    request_parts = [requests[i * part : (i + 1) * part] for i in range(parts)]
    arrived, tables, request_parts = barrier((arrived, tables, request_parts))

    tenants = [block[each * rows, width : width + each] for block in arrived]
    tenants = jnp.concatenate(tenants).astype(jnp.int32)
    tenant_row, tenant_slot = tenants // span, tenants % owned
    place = ((row - tenant_row) % rows_dp) * owned + tenant_slot
    partial = low(place, tables, firsts, arrived, rank, rows)
    target = ((tenant_row - row) % rows_dp) * owned + tenant_slot
    sums = grad(target, tensor_parts(partial), arrived, rank, rows, rows_dp)
    pieces = [sums[0], *ring_reduce(sums, rows_dp)]

    tenant_ids = jnp.arange(tenant_group.shape[0], dtype=jnp.int32)
    served = (tenant_group == group).astype(jnp.int32)
    by_row = served.reshape(rows_dp, span)
    slot_of = jnp.cumsum(by_row, axis=1) - by_row
    mine = lax.dynamic_slice_in_dim(by_row, row, 1, 0)[0]
    mine_slot = lax.dynamic_slice_in_dim(slot_of, row, 1, 0)[0]
    position = jnp.arange(span, dtype=jnp.int32)
    relative = ((group - position // owned) % groups) * owned + position % owned
    wanted = jnp.sum(
        jnp.where(
            (mine[None, :] == 1)
            & (mine_slot[None, :] == jnp.arange(owned, dtype=jnp.int32)[:, None]),
            relative[None, :],
            0,
        ),
        axis=1,
        dtype=jnp.int32,
    )
    slot_here = ((row - tenant_ids // span) % rows_dp) * owned + slot_of.reshape(-1)
    slot_here = jnp.where(served == 1, slot_here, -1)
    request_slot = jnp.sum(
        jnp.where(request_adapter[0][:, None] == tenant_ids[None, :], slot_here[None, :], 0),
        axis=1,
        dtype=jnp.int32,
    )
    count = requests.shape[0] * steps
    slots = jnp.broadcast_to(request_slot[:, None], (requests.shape[0], steps)).reshape(1, count)
    *new, fresh = adam(
        pieces,
        [flat(x) for x in (adapter_a, moment_a, second_a)],
        [flat(x) for x in (adapter_b, moment_b, second_b)],
    )
    in_row = spread(fresh, "group")
    fresh, wanted, slots, request_parts = barrier((fresh, wanted, slots, request_parts))
    frozen = [
        jnp.einsum("qsd,dk->qsk", x, dec_weight, preferred_element_type=F32).reshape(
            part * steps, width_b
        )
        for x in request_parts
    ]
    frozen = jnp.concatenate(frozen)
    x_slice = lax.dynamic_slice_in_dim(requests, lax.axis_index("tensor") * width, width, 2)
    x_slice = x_slice.reshape(count, width)
    in_row, wanted, slots, frozen, x_slice = barrier((in_row, wanted, slots, frozen, x_slice))
    own = pick(wanted, in_row, rank)
    served_fresh, firsts = ring(own, rows_dp, owned, rank)

    dec_part = decode_in(slots, x_slice, served_fresh, firsts, rank)
    decoded = decode_out(slots, frozen, tensor_parts(dec_part), served_fresh, firsts, rank)
    new_a = [x.reshape(adapter_a.shape) for x in new[:3]]
    new_b = [x.reshape(adapter_b.shape) for x in new[3:]]
    return (
        new_a[0],
        new_b[0],
        new_a[1],
        new_b[1],
        new_a[2],
        new_b[2],
        decoded.reshape((1,) + requests.shape[:2] + (width_b,)),
    )


def solution(mesh):
    state = P(("dp", "group"), None, "tensor")
    return jax.shard_map(
        local,
        mesh=mesh,
        in_specs=(
            P(("dp", "group"), "tensor"),
            P(("dp", "group"), "tensor"),
            P(("dp", "group")),
            P(("dp", "group")),
            state,
            state,
            state,
            state,
            state,
            state,
            P(),
            P("group", "dp", None, None),
            P(None, "tensor"),
            P("group", "dp"),
        ),
        out_specs=(
            state,
            state,
            state,
            state,
            state,
            state,
            P("group", "dp", None, "tensor"),
        ),
        check_vma=False,
    )
```

```python
import functools

import jax
import jax.numpy as jnp
from jax import lax
from jax.experimental import pallas as pl
from jax.experimental.pallas import tpu as pltpu
from jax.sharding import PartitionSpec as P

STEP_NUM = 10

adapter_scale = 2.0
beta_one = 0.9
beta_two = 0.999
step_rate = 0.001
adam_eps = 1e-08

BF = jnp.bfloat16
F32 = jnp.float32
MIB = 1024 * 1024


def dot(a, b, dims):
    return lax.dot_general(a, b, (dims, ((), ())), preferred_element_type=F32)


def shift(x, axis, distance):
    size = lax.axis_size(axis)
    return lax.ppermute(x, axis, [(i, (i + distance) % size) for i in range(size)])


def spread(x, axis):
    return [x] + [shift(x, axis, d) for d in range(1, lax.axis_size(axis))]


def ring(x, size, owned):
    ahead = behind = x
    arrays, firsts = [x], [0]
    for hop in range(1, size // 2 + 1):
        ahead = shift(ahead, "dp", 1)
        arrays.append(ahead)
        firsts.append(hop * owned)
        if hop < size // 2:
            behind = shift(behind, "dp", -1)
            arrays.append(behind)
            firsts.append((size - hop) * owned)
    return arrays, firsts


def two_stage(x, size, owned):
    near = [shift(x, "dp", d) for d in (1, -1, 2, -2)]
    far = [shift(near[2], "dp", 1), shift(near[3], "dp", -1), shift(near[2], "dp", 2)]
    firsts = [d % size * owned for d in (0, 1, -1, 2, -2, 3, -3, 4)]
    return [x, *near, *far], firsts


def two_stage_reduce(x, size):
    upper, lower = x[size // 2], x[-1]
    half = upper.shape[0]
    after = [shift(x[3], "dp", 1), shift(upper, "dp", 2)]
    before = [shift(x[5], "dp", -1), shift(lower, "dp", -2)]
    ahead = jnp.concatenate(
        [add(x[2][:half], after[0][:half], after[1]), add(x[2][half:], after[0][half:])]
    )
    behind = jnp.concatenate(
        [add(x[6][:half], before[0][:half]), add(x[6][half:], before[0][half:], before[1])]
    )
    near = [shift(x[1], "dp", 1), shift(x[7], "dp", -1)]
    return [*near, shift(ahead, "dp", 2), shift(behind, "dp", -2)]


def spot(memory, n=1):
    return [pl.BlockSpec(memory_space=memory)] * n


vmem = functools.partial(spot, pltpu.VMEM)
smem = functools.partial(spot, pltpu.SMEM)
anywhere = functools.partial(spot, pl.ANY)
SMALL = pltpu.CompilerParams(vmem_limit_bytes=14 * MIB)
LARGE = pltpu.CompilerParams(vmem_limit_bytes=61 * MIB)


def shape(dims, dtype=BF):
    return jax.ShapeDtypeStruct(dims, dtype)


def block_of(ref, index, rows):
    return ref.at[pl.ds(pl.multiple_of(index * rows, rows), rows), :]


def fetch(refs, rooms, sems):
    copies = [
        pltpu.make_async_copy(ref, room, sems.at[i]) for i, (ref, room) in enumerate(zip(refs, rooms))
    ]
    for copy in copies:
        copy.start()
    return copies


def begin_kernel(rows, groups, tenant, count, x, dy, *refs):
    packs, refs = refs[:groups], refs[groups:]
    source, ids, dy_here, room, sems, x_sems, out_sems = refs
    blocks = 2 * groups
    width = x.shape[1]
    loads = fetch([dy], [dy_here], sems)
    group = lax.axis_index("group")
    names = [tenant[b] for b in range(blocks)]
    far = [lax.rem(lax.rem(name // 2, groups) - group + groups, groups) for name in names]
    for b in range(blocks):
        place = 2 * far[b]
        for e in range(b):
            place += (far[e] == far[b]).astype(jnp.int32)
        source[place] = b
        ids[place] = names[b]
    moves = []
    for s in range(blocks):
        part = pl.ds((s % 2) * rows, rows)
        moves.append(
            pltpu.make_async_copy(
                block_of(x, source[s], rows), room.at[s // 2, part, :width], x_sems.at[s]
            )
        )
        moves[-1].start()
    loads[0].wait()
    for s in range(blocks):
        block = block_of(dy_here, source[s], rows)[...].astype(F32)
        live = lax.broadcasted_iota(jnp.int32, block.shape, 0) < count[source[s]]
        block = jnp.where(live, block, 0.0).astype(BF)
        room[s // 2, (s % 2) * rows : (s % 2 + 1) * rows, width:] = block
    stores = []
    for d in range(groups):
        lane = lax.broadcasted_iota(jnp.int32, (16, dy.shape[1]), 1)
        both = jnp.where(lane == 0, ids[2 * d], ids[2 * d + 1])
        room[d, 2 * rows :, width:] = both.astype(F32).astype(BF)
        room[d, 2 * rows :, :width] = jnp.zeros((16, width), BF)
        moves[2 * d].wait()
        moves[2 * d + 1].wait()
        stores.append(pltpu.make_async_copy(room.at[d], packs[d], out_sems.at[d]))
        stores[-1].start()
    for store in stores:
        store.wait()


def begin(tenant, count, x, dy, groups):
    rows = x.shape[0] // tenant.shape[0]
    wide = x.shape[1] + dy.shape[1]
    return pl.pallas_call(
        functools.partial(begin_kernel, rows, groups),
        in_specs=smem(2) + anywhere(2),
        out_specs=anywhere(groups),
        out_shape=[shape((2 * rows + 16, wide))] * groups,
        scratch_shapes=[
            pltpu.SMEM((2 * groups,), jnp.int32),
            pltpu.SMEM((2 * groups,), jnp.int32),
            pltpu.VMEM(dy.shape, BF),
            pltpu.VMEM((groups, 2 * rows + 16, wide), BF),
            pltpu.SemaphoreType.DMA((1,)),
            pltpu.SemaphoreType.DMA((2 * groups,)),
            pltpu.SemaphoreType.DMA((groups,)),
        ],
        compiler_params=LARGE,
    )(tenant, count, x, dy)


def frozen_kernel(tensor, x, weight, out, x_out):
    step = pl.program_id(0)
    width = x_out.shape[1]
    pieces = x.shape[2] // width
    block = x[...].reshape(out.shape[0], x.shape[2])

    @pl.when(step == 0)
    def _():
        out[...] = jnp.zeros_like(out)

    out[...] += dot(block, weight[...], ((1,), (0,)))
    for i in range(pieces):

        @pl.when(tensor[0] == step * pieces + i)
        def _():
            x_out[...] = block[:, i * width : (i + 1) * width]


def frozen(tensor, requests, weight, part, parts, width):
    count = requests.shape[0] // parts
    steps = requests.shape[1]
    width_b = weight.shape[1]
    wide = 4 * width
    return pl.pallas_call(
        frozen_kernel,
        grid_spec=pltpu.PrefetchScalarGridSpec(
            num_scalar_prefetch=1,
            grid=(requests.shape[2] // wide,),
            in_specs=[
                pl.BlockSpec((count, steps, wide), lambda k, tensor: (part, 0, k)),
                pl.BlockSpec((wide, width_b), lambda k, tensor: (k, 0)),
            ],
            out_specs=[
                pl.BlockSpec((count * steps, width_b), lambda k, tensor: (0, 0)),
                pl.BlockSpec((count * steps, width), lambda k, tensor: (0, 0)),
            ],
        ),
        out_shape=[shape((count * steps, width_b), F32), shape((count * steps, width))],
        compiler_params=LARGE,
    )(tensor, requests, weight)


def low_kernel(rank, rows, size, owned, firsts, *refs):
    parts = len(firsts)
    tables, refs = refs[:parts], refs[parts:]
    *blocks, out, names, table, here, sems = refs
    wide = table.shape[1]
    width = wide - 128
    row = lax.axis_index("dp")
    span = owned * len(blocks)
    used = 2 * rows
    rooms = [
        table.at[first * rank : first * rank + ref.shape[0], :] for first, ref in zip(firsts, tables)
    ]
    rooms += [here.at[d] for d in range(len(blocks))]
    copies = fetch([*tables, *blocks], rooms, sems)
    for copy in copies[:parts]:
        copy.wait()
    half = used // rows * len(blocks) * rank
    for s in range(2 * len(blocks)):
        if s % 2 == 0:
            copies[parts + s // 2].wait()
            ids = here[s // 2, used : used + 16, width:].astype(F32)
        name = ids[0, s % 2].astype(jnp.int32)
        place = lax.rem(row - name // span + size, size) * owned + lax.rem(name, owned)
        names[s] = name
        block = here[s // 2, (s % 2) * rows : (s % 2 + 1) * rows, :]
        chosen = block_of(table, place, rank)[...]
        low_in = dot(chosen[:, :width], block[:, :width], ((1,), (1,)))
        low_back = dot(chosen[:, width:], block[:, width:], ((1,), (1,)))
        out[s * rank : (s + 1) * rank, :] = low_in.astype(BF)
        out[half + s * rank : half + (s + 1) * rank, :] = low_back.astype(BF)


def low(tables, firsts, blocks, rank, rows, size, owned):
    wide = blocks[0].shape[1]
    total = sum(table.shape[0] for table in tables)
    return pl.pallas_call(
        functools.partial(low_kernel, rank, rows, size, owned, firsts),
        in_specs=anywhere(len(tables) + len(blocks)),
        out_specs=vmem() + smem(),
        out_shape=[
            shape((4 * len(blocks) * rank, rows)),
            shape((2 * len(blocks),), jnp.int32),
        ],
        scratch_shapes=[
            pltpu.VMEM((total, wide), BF),
            pltpu.VMEM((len(blocks),) + blocks[0].shape, BF),
            pltpu.SemaphoreType.DMA((len(tables) + len(blocks),)),
        ],
        compiler_params=LARGE,
    )(*tables, *blocks)


def added(refs):
    total = refs[0][...].astype(F32)
    for ref in refs[1:]:
        total = total + ref[...].astype(F32)
    return total


def grad_kernel(rank, rows, parts, owned, names, *refs):
    lows, refs = refs[:parts], refs[parts:]
    groups = lows[0].shape[0] // (4 * rank)
    blocks, refs = refs[:groups], refs[groups:]
    *outs, sums, lows_here, here, half, sems, out_sems = refs
    width = sums.shape[2] - 128
    row = lax.axis_index("dp")
    span, size = owned * groups, len(outs) - 1
    copies = fetch(
        [*lows, *[ref.at[: 2 * rows, :] for ref in blocks]],
        [*[lows_here.at[d] for d in range(parts)], *[here.at[d] for d in range(groups)]],
        sems,
    )
    sums[...] = jnp.zeros_like(sums)
    for copy in copies[:parts]:
        copy.wait()
    total = added([lows_here.at[d] for d in range(parts)]).astype(BF)
    middle = 2 * groups * rank
    for s in range(2 * groups):
        if s % 2 == 0:
            copies[parts + s // 2].wait()
        block = here[s // 2, (s % 2) * rows : (s % 2 + 1) * rows, :]
        low_in = total[s * rank : (s + 1) * rank]
        low_back = total[middle + s * rank : middle + (s + 1) * rank]
        name = names[s]
        place = lax.rem(name // span - row + size, size) * owned + lax.rem(name, owned)
        sums[place, :, :width] += dot(low_back, block[:, :width], ((1,), (0,)))
        sums[place, :, width:] += dot(low_in, block[:, width:], ((1,), (0,)))
    stores = []
    far = size // 2
    order = [3, 5, far, 2, 6, 1, 7, 0]
    for d in order:
        for j in range(2):
            half[d, j * rank : (j + 1) * rank, :] = (adapter_scale * sums[2 * d + j]).astype(BF)
        if d == far:
            ends = [(half.at[d, :rank], outs[far]), (half.at[d, rank:], outs[-1])]
        else:
            ends = [(half.at[d], outs[d])]
        for source, out in ends:
            stores.append(pltpu.make_async_copy(source, out, out_sems.at[len(stores)]))
            stores[-1].start()
    for store in stores:
        store.wait()


def grad(names, lows, blocks, rank, rows, targets, owned):
    wide = blocks[0].shape[1]
    return pl.pallas_call(
        functools.partial(grad_kernel, rank, rows, len(lows), owned),
        in_specs=smem() + anywhere(len(lows) + len(blocks)),
        out_specs=anywhere(targets + 1),
        out_shape=[
            shape((rank if d in (targets // 2, targets) else 2 * rank, wide))
            for d in range(targets + 1)
        ],
        scratch_shapes=[
            pltpu.VMEM((2 * targets, rank, wide), F32),
            pltpu.VMEM((len(lows),) + lows[0].shape, BF),
            pltpu.VMEM((len(blocks), 2 * rows, wide), BF),
            pltpu.VMEM((targets, 2 * rank, wide), BF),
            pltpu.SemaphoreType.DMA((len(lows) + len(blocks),)),
            pltpu.SemaphoreType.DMA((targets + 1,)),
        ],
        compiler_params=LARGE,
    )(names, *lows, *blocks)


def adam_update(weights, moment, second, gradient):
    moment_new = beta_one * moment + (1.0 - beta_one) * gradient
    second_new = beta_two * second + (1.0 - beta_two) * gradient * gradient
    unbiased_m = moment_new / (1.0 - beta_one**STEP_NUM)
    unbiased_v = second_new / (1.0 - beta_two**STEP_NUM)
    weights_new = weights - step_rate * unbiased_m / (jnp.sqrt(unbiased_v) + adam_eps)
    return (weights_new, moment_new, second_new)


def adam_kernel(parts, *refs):
    grads, refs = refs[:parts], refs[parts:]
    states, outs, refs = refs[:6], refs[6:13], refs[13:]
    here, olds, news, fresh, sems, out_sems = refs[0], refs[1:7], refs[7:13], *refs[13:]
    copies = fetch([*states, *grads], [*olds, *[here.at[d] for d in range(parts)]], sems)
    width = olds[0].shape[1]
    for copy in copies:
        copy.wait()
    total = added([here.at[d] for d in range(parts)])
    for first, cols in ((0, slice(0, width)), (3, slice(width, None))):
        values = adam_update(*[ref[...] for ref in olds[first : first + 3]], total[:, cols])
        for ref, value in zip(news[first : first + 3], values):
            ref[...] = value
        fresh[:, cols] = values[0].astype(BF)
    for store in fetch([*news, fresh], outs, out_sems):
        store.wait()


def adam(grads, state_a, state_b):
    rows, width = state_a[0].shape
    width_b = state_b[0].shape[1]
    wide = width + width_b
    states = [pltpu.VMEM((rows, width), F32)] * 3 + [pltpu.VMEM((rows, width_b), F32)] * 3
    return pl.pallas_call(
        functools.partial(adam_kernel, len(grads)),
        in_specs=anywhere(len(grads) + 6),
        out_specs=anywhere(7),
        out_shape=[shape((rows, width), F32)] * 3
        + [shape((rows, width_b), F32)] * 3
        + [shape((rows, wide))],
        scratch_shapes=[pltpu.VMEM((len(grads), rows, wide), BF)]
        + states
        + states
        + [
            pltpu.VMEM((rows, wide), BF),
            pltpu.SemaphoreType.DMA((len(grads) + 6,)),
            pltpu.SemaphoreType.DMA((7,)),
        ],
        compiler_params=LARGE,
    )(*grads, *state_a, *state_b)


def pick_kernel(rank, index, *refs):
    *refs, out = refs
    for i in range(2):
        device, slot = index[i] // 2, index[i] % 2
        for d, ref in enumerate(refs):

            @pl.when(device == d)
            def _():
                out[i * rank : (i + 1) * rank, :] = block_of(ref, slot, rank)[...]


def pick(index, arrays, rank):
    return pl.pallas_call(
        functools.partial(pick_kernel, rank),
        in_specs=smem(1) + vmem(len(arrays)),
        out_specs=vmem()[0],
        out_shape=shape(arrays[0].shape),
        compiler_params=SMALL,
    )(index, *arrays)


def decode_in_kernel(rank, firsts, parts, slots, *refs):
    xs, refs = refs[:parts], refs[parts:]
    *refs, out = refs
    width = xs[0].shape[1]
    count = xs[0].shape[0]
    for i, x in enumerate(xs):
        here = slots[:, i * count : (i + 1) * count]
        total = jnp.zeros((rank, count), F32)
        for first, ref in zip(firsts, refs):
            both = dot(ref[:, :width], x[...], ((1,), (1,)))
            for j in range(ref.shape[0] // rank):
                total += jnp.where(here == first + j, both[j * rank : (j + 1) * rank], 0.0)
        out[:, i * count : (i + 1) * count] = total


def decode_in(slots, xs, fresh, firsts, rank):
    return pl.pallas_call(
        functools.partial(decode_in_kernel, rank, firsts, len(xs)),
        in_specs=vmem(1 + len(xs) + len(fresh)),
        out_specs=vmem()[0],
        out_shape=shape((rank, slots.shape[1]), F32),
        compiler_params=SMALL,
    )(slots, *xs, *fresh)


def decode_out_kernel(rank, parts, firsts, slots, *refs):
    frozen, refs = refs[:2], refs[2:]
    lows, fresh, out = refs[:parts], refs[parts:-1], refs[-1]
    width_b = out.shape[1]
    total = added(lows).astype(BF).astype(F32)
    result = jnp.concatenate([ref[...] for ref in frozen], axis=0)
    for first, ref in zip(firsts, fresh):
        wide = ref.shape[1]
        both = jnp.concatenate(
            [jnp.where(slots[...] == first + j, total, 0.0) for j in range(ref.shape[0] // rank)],
            axis=0,
        )
        part = dot(both.T.astype(BF), ref[:, wide - width_b :], ((1,), (0,)))
        result += adapter_scale * part
    out[...] = result.astype(BF)


def decode_out(slots, frozen, lows, fresh, firsts, rank):
    return pl.pallas_call(
        functools.partial(decode_out_kernel, rank, len(lows), firsts),
        in_specs=vmem(1 + len(frozen) + len(lows) + len(fresh)),
        out_specs=vmem()[0],
        out_shape=shape((slots.shape[1], frozen[0].shape[1])),
        compiler_params=SMALL,
    )(slots, *frozen, *lows, *fresh)


def add(x, *more):
    total = x.astype(F32)
    for y in more:
        total = total + y.astype(F32)
    return total.astype(x.dtype)


def tensor_parts(x):
    size = lax.axis_size("tensor")
    x = add(x, lax.ppermute(x, "tensor", [(i, i ^ 1) for i in range(size)]))
    return [x] + [
        lax.ppermute(x, "tensor", [(i, (i + 2 * d) % size) for i in range(size)])
        for d in range(1, size // 2)
    ]


def local(
    learn_x,
    learn_dy,
    block_tenant,
    block_count,
    adapter_a,
    adapter_b,
    moment_a,
    moment_b,
    second_a,
    second_b,
    tenant_group,
    decode_inputs,
    dec_weight,
    request_adapter,
):
    groups = lax.axis_size("group")
    rows_dp = lax.axis_size("dp")
    group = lax.axis_index("group")
    row = lax.axis_index("dp")
    owned, rank, width = adapter_a.shape
    width_b = adapter_b.shape[2]
    span = groups * owned
    barrier = lax.optimization_barrier

    def flat(x):
        return x.reshape(owned * rank, x.shape[2])

    blocks = block_tenant.shape[0]
    rows = learn_x.shape[0] // blocks
    packed = begin(block_tenant, block_count, learn_x, learn_dy, groups)
    packed, state = barrier((packed, (adapter_a, adapter_b)))
    arrived = [packed[0]] + [shift(packed[d], "group", d) for d in range(1, groups)]
    own = jnp.concatenate([flat(x).astype(BF) for x in state], axis=1)
    tables, firsts = ring(own, rows_dp, owned)
    requests = decode_inputs[0]
    steps = requests.shape[1]
    tensor = lax.axis_index("tensor").reshape(1)
    tables, requests = barrier((tables, requests))
    early = frozen(tensor, requests, dec_weight, 0, 2, width)
    arrived, tables, early = barrier((arrived, tables, early))

    partial, names = low(tables, firsts, arrived, rank, rows, rows_dp, owned)
    sums = grad(names, tensor_parts(partial), arrived, rank, rows, rows_dp, owned)
    pieces = [sums[0], *two_stage_reduce(sums, rows_dp)]
    *new, fresh = adam(
        pieces,
        [flat(x) for x in (adapter_a, moment_a, second_a)],
        [flat(x) for x in (adapter_b, moment_b, second_b)],
    )

    tenant_ids = jnp.arange(tenant_group.shape[0], dtype=jnp.int32)
    served = (tenant_group == group).astype(jnp.int32)
    by_row = served.reshape(rows_dp, span)
    slot_of = jnp.cumsum(by_row, axis=1) - by_row
    mine = lax.dynamic_slice_in_dim(by_row, row, 1, 0)[0]
    mine_slot = lax.dynamic_slice_in_dim(slot_of, row, 1, 0)[0]
    position = jnp.arange(span, dtype=jnp.int32)
    relative = ((group - position // owned) % groups) * owned + position % owned
    wanted = jnp.sum(
        jnp.where(
            (mine[None, :] == 1)
            & (mine_slot[None, :] == jnp.arange(owned, dtype=jnp.int32)[:, None]),
            relative[None, :],
            0,
        ),
        axis=1,
        dtype=jnp.int32,
    )
    slot_here = ((row - tenant_ids // span) % rows_dp) * owned + slot_of.reshape(-1)
    slot_here = jnp.where(served == 1, slot_here, -1)
    request_slot = jnp.sum(
        jnp.where(request_adapter[0][:, None] == tenant_ids[None, :], slot_here[None, :], 0),
        axis=1,
        dtype=jnp.int32,
    )
    count = requests.shape[0] * steps
    slots = jnp.broadcast_to(request_slot[:, None], (requests.shape[0], steps)).reshape(1, count)
    *new, fresh = adam(
        pieces,
        [flat(x) for x in (adapter_a, moment_a, second_a)],
        [flat(x) for x in (adapter_b, moment_b, second_b)],
    )
    in_row = spread(fresh, "group")
    fresh, wanted, slots, requests = barrier((fresh, wanted, slots, requests))
    late = frozen(tensor, requests, dec_weight, 1, 2, width)
    in_row, wanted, slots, late = barrier((in_row, wanted, slots, late))
    served_fresh, firsts = two_stage(pick(wanted, in_row, rank), rows_dp, owned)

    dec_part = decode_in(slots, [early[1], late[1]], served_fresh, firsts, rank)
    decoded = decode_out(
        slots, [early[0], late[0]], tensor_parts(dec_part), served_fresh, firsts, rank
    )
    new_a = [x.reshape(adapter_a.shape) for x in new[:3]]
    new_b = [x.reshape(adapter_b.shape) for x in new[3:]]
    return (
        new_a[0],
        new_b[0],
        new_a[1],
        new_b[1],
        new_a[2],
        new_b[2],
        decoded.reshape((1,) + requests.shape[:2] + (width_b,)),
    )


def solution(mesh):
    state = P(("dp", "group"), None, "tensor")
    return jax.shard_map(
        local,
        mesh=mesh,
        in_specs=(
            P(("dp", "group"), "tensor"),
            P(("dp", "group"), "tensor"),
            P(("dp", "group")),
            P(("dp", "group")),
            state,
            state,
            state,
            state,
            state,
            state,
            P(),
            P("group", "dp", None, None),
            P(None, "tensor"),
            P("group", "dp"),
        ),
        out_specs=(
            state,
            state,
            state,
            state,
            state,
            state,
            P("group", "dp", None, "tensor"),
        ),
        check_vma=False,
    )
```

```python
import functools

import jax
import jax.numpy as jnp
from jax import lax
from jax.experimental import pallas as pl
from jax.experimental.pallas import tpu as pltpu
from jax.sharding import PartitionSpec as P

STEP_NUM = 10

adapter_scale = 2.0
beta_one = 0.9
beta_two = 0.999
step_rate = 0.001
adam_eps = 1e-08

BF = jnp.bfloat16
F32 = jnp.float32
MIB = 1024 * 1024


def dot(a, b, dims):
    return lax.dot_general(a, b, (dims, ((), ())), preferred_element_type=F32)


def shift(x, axis, distance):
    size = lax.axis_size(axis)
    return lax.ppermute(x, axis, [(i, (i + distance) % size) for i in range(size)])


def spread(x, axis):
    return [x] + [shift(x, axis, d) for d in range(1, lax.axis_size(axis))]


def ring(x, size, owned):
    ahead = behind = x
    arrays, firsts = [x], [0]
    for hop in range(1, size // 2 + 1):
        ahead = shift(ahead, "dp", 1)
        arrays.append(ahead)
        firsts.append(hop * owned)
        if hop < size // 2:
            behind = shift(behind, "dp", -1)
            arrays.append(behind)
            firsts.append((size - hop) * owned)
    return arrays, firsts


def two_stage(x, size, owned):
    near = [shift(x, "dp", d) for d in (1, -1, 2, -2)]
    far = [shift(near[2], "dp", 1), shift(near[3], "dp", -1), shift(near[2], "dp", 2)]
    firsts = [d % size * owned for d in (0, 1, -1, 2, -2, 3, -3, 4)]
    return [x, *near, *far], firsts


def two_stage_reduce(x, size):
    upper, lower = x[size // 2], x[-1]
    half = upper.shape[0]
    after, before = shift(x[3], "dp", 1), shift(x[5], "dp", -1)
    far_after, far_before = shift(upper, "dp", 2), shift(lower, "dp", -2)
    after, before, one, other = lax.optimization_barrier((after, before, x[1], x[7]))
    near = [shift(one, "dp", 1), shift(other, "dp", -1)]
    ahead = jnp.concatenate(
        [add(x[2][:half], after[:half], far_after), add(x[2][half:], after[half:])]
    )
    behind = jnp.concatenate(
        [add(x[6][:half], before[:half]), add(x[6][half:], before[half:], far_before)]
    )
    return [*near, shift(ahead, "dp", 2), shift(behind, "dp", -2)]


def spot(memory, n=1):
    return [pl.BlockSpec(memory_space=memory)] * n


vmem = functools.partial(spot, pltpu.VMEM)
smem = functools.partial(spot, pltpu.SMEM)
anywhere = functools.partial(spot, pl.ANY)
SMALL = pltpu.CompilerParams(vmem_limit_bytes=14 * MIB)
MIDDLE = pltpu.CompilerParams(vmem_limit_bytes=52 * MIB)
LARGE = pltpu.CompilerParams(vmem_limit_bytes=61 * MIB)


def shape(dims, dtype=BF):
    return jax.ShapeDtypeStruct(dims, dtype)


def block_of(ref, index, rows):
    return ref.at[pl.ds(pl.multiple_of(index * rows, rows), rows), :]


def fetch(refs, rooms, sems):
    copies = [
        pltpu.make_async_copy(ref, room, sems.at[i]) for i, (ref, room) in enumerate(zip(refs, rooms))
    ]
    for copy in copies:
        copy.start()
    return copies


def begin_kernel(rows, groups, tenant, count, x, dy, *refs):
    packs, refs = refs[:groups], refs[groups:]
    source, ids, dy_here, room, sems, x_sems, out_sems = refs
    blocks = 2 * groups
    width = x.shape[1]
    loads = fetch([dy], [dy_here], sems)
    group = lax.axis_index("group")
    names = [tenant[b] for b in range(blocks)]
    far = [lax.rem(lax.rem(name // 2, groups) - group + groups, groups) for name in names]
    for b in range(blocks):
        place = 2 * far[b]
        for e in range(b):
            place += (far[e] == far[b]).astype(jnp.int32)
        source[place] = b
        ids[place] = names[b]
    moves = []
    for s in range(blocks):
        part = pl.ds((s % 2) * rows, rows)
        moves.append(
            pltpu.make_async_copy(
                block_of(x, source[s], rows), room.at[s // 2, part, :width], x_sems.at[s]
            )
        )
        moves[-1].start()
    loads[0].wait()
    for s in range(blocks):
        block = block_of(dy_here, source[s], rows)[...].astype(F32)
        live = lax.broadcasted_iota(jnp.int32, block.shape, 0) < count[source[s]]
        block = jnp.where(live, block, 0.0).astype(BF)
        room[s // 2, (s % 2) * rows : (s % 2 + 1) * rows, width:] = block
    stores = []
    for d in range(groups):
        lane = lax.broadcasted_iota(jnp.int32, (16, dy.shape[1]), 1)
        both = jnp.where(lane == 0, ids[2 * d], ids[2 * d + 1])
        room[d, 2 * rows :, width:] = both.astype(F32).astype(BF)
        room[d, 2 * rows :, :width] = jnp.zeros((16, width), BF)
        moves[2 * d].wait()
        moves[2 * d + 1].wait()
        stores.append(pltpu.make_async_copy(room.at[d], packs[d], out_sems.at[d]))
        stores[-1].start()
    for store in stores:
        store.wait()


def begin(tenant, count, x, dy, groups):
    rows = x.shape[0] // tenant.shape[0]
    wide = x.shape[1] + dy.shape[1]
    return pl.pallas_call(
        functools.partial(begin_kernel, rows, groups),
        in_specs=smem(2) + anywhere(2),
        out_specs=anywhere(groups),
        out_shape=[shape((2 * rows + 16, wide))] * groups,
        scratch_shapes=[
            pltpu.SMEM((2 * groups,), jnp.int32),
            pltpu.SMEM((2 * groups,), jnp.int32),
            pltpu.VMEM(dy.shape, BF),
            pltpu.VMEM((groups, 2 * rows + 16, wide), BF),
            pltpu.SemaphoreType.DMA((1,)),
            pltpu.SemaphoreType.DMA((2 * groups,)),
            pltpu.SemaphoreType.DMA((groups,)),
        ],
        compiler_params=LARGE,
    )(tenant, count, x, dy)


def frozen_kernel(tensor, x, weight, out, x_out):
    step = pl.program_id(0)
    width = x_out.shape[1]
    pieces = x.shape[2] // width
    block = x[...].reshape(out.shape[0], x.shape[2])

    @pl.when(step == 0)
    def _():
        out[...] = jnp.zeros_like(out)

    out[...] += dot(block, weight[...], ((1,), (0,)))
    for i in range(pieces):

        @pl.when(tensor[0] == step * pieces + i)
        def _():
            x_out[...] = block[:, i * width : (i + 1) * width]


def frozen(tensor, requests, weight, part, parts, width, params):
    count = requests.shape[0] // parts
    steps = requests.shape[1]
    width_b = weight.shape[1]
    wide = 4 * width
    return pl.pallas_call(
        frozen_kernel,
        grid_spec=pltpu.PrefetchScalarGridSpec(
            num_scalar_prefetch=1,
            grid=(requests.shape[2] // wide,),
            in_specs=[
                pl.BlockSpec((count, steps, wide), lambda k, tensor: (part, 0, k)),
                pl.BlockSpec((wide, width_b), lambda k, tensor: (k, 0)),
            ],
            out_specs=[
                pl.BlockSpec((count * steps, width_b), lambda k, tensor: (0, 0)),
                pl.BlockSpec((count * steps, width), lambda k, tensor: (0, 0)),
            ],
        ),
        out_shape=[shape((count * steps, width_b), F32), shape((count * steps, width))],
        compiler_params=params,
    )(tensor, requests, weight)


def low_kernel(rank, rows, size, owned, firsts, *refs):
    parts = len(firsts)
    tables, refs = refs[:parts], refs[parts:]
    *blocks, mine, his, names, table, here, both, sems = refs
    core = lax.rem(lax.axis_index("tensor"), 2)
    wide = table.shape[1]
    width = wide - 128
    row = lax.axis_index("dp")
    span = owned * len(blocks)
    used = 2 * rows
    rooms = [
        table.at[first * rank : first * rank + ref.shape[0], :] for first, ref in zip(firsts, tables)
    ]
    rooms += [here.at[d] for d in range(len(blocks))]
    copies = fetch([*tables, *blocks], rooms, sems)
    for copy in copies[:parts]:
        copy.wait()
    for s in range(2 * len(blocks)):
        if s % 2 == 0:
            copies[parts + s // 2].wait()
            ids = here[s // 2, used : used + 16, width:].astype(F32)
        name = ids[0, s % 2].astype(jnp.int32)
        place = lax.rem(row - name // span + size, size) * owned + lax.rem(name, owned)
        names[s] = name
        block = here[s // 2, (s % 2) * rows : (s % 2 + 1) * rows, :]
        chosen = block_of(table, place, rank)[...]
        low_in = dot(chosen[:, :width], block[:, :width], ((1,), (1,)))
        low_back = dot(chosen[:, width:], block[:, width:], ((1,), (1,)))
        both[0, s * rank : (s + 1) * rank, :] = low_in.astype(BF)
        both[1, s * rank : (s + 1) * rank, :] = low_back.astype(BF)
    mine[...] = both[core]
    his[...] = both[1 - core]


def low(tables, firsts, blocks, rank, rows, size, owned):
    wide = blocks[0].shape[1]
    total = sum(table.shape[0] for table in tables)
    return pl.pallas_call(
        functools.partial(low_kernel, rank, rows, size, owned, firsts),
        in_specs=anywhere(len(tables) + len(blocks)),
        out_specs=vmem(2) + smem(),
        out_shape=[
            shape((2 * len(blocks) * rank, rows)),
            shape((2 * len(blocks) * rank, rows)),
            shape((2 * len(blocks),), jnp.int32),
        ],
        scratch_shapes=[
            pltpu.VMEM((total, wide), BF),
            pltpu.VMEM((len(blocks),) + blocks[0].shape, BF),
            pltpu.VMEM((2, 2 * len(blocks) * rank, rows), BF),
            pltpu.SemaphoreType.DMA((len(tables) + len(blocks),)),
        ],
        compiler_params=LARGE,
    )(*tables, *blocks)


def added(refs):
    total = refs[0][...].astype(F32)
    for ref in refs[1:]:
        total = total + ref[...].astype(F32)
    return total


def grad_kernel(rank, rows, parts, owned, names, *refs):
    lows, refs = refs[:parts], refs[parts:]
    groups = lows[0].shape[0] // (2 * rank)
    core = lax.rem(lax.axis_index("tensor"), 2)
    blocks, refs = refs[:groups], refs[groups:]
    *outs, sums, lows_here, here, half, sems, out_sems = refs
    width = sums.shape[2] - 128
    row = lax.axis_index("dp")
    span, size = owned * groups, len(outs) - 1
    copies = fetch(
        [*lows, *[ref.at[: 2 * rows, :] for ref in blocks]],
        [*[lows_here.at[d] for d in range(parts)], *[here.at[d] for d in range(groups)]],
        sems,
    )
    sums[...] = jnp.zeros_like(sums)
    for copy in copies[:parts]:
        copy.wait()
    for s in range(2 * groups):
        if s % 2 == 0:
            copies[parts + s // 2].wait()
        block = here[s // 2, (s % 2) * rows : (s % 2 + 1) * rows, :]
        low_in = lows_here[core, s * rank : (s + 1) * rank, :]
        low_back = lows_here[1 - core, s * rank : (s + 1) * rank, :]
        name = names[s]
        place = lax.rem(name // span - row + size, size) * owned + lax.rem(name, owned)
        sums[place, :, :width] += dot(low_back, block[:, :width], ((1,), (0,)))
        sums[place, :, width:] += dot(low_in, block[:, width:], ((1,), (0,)))
    stores = []
    far = size // 2
    order = [3, 5, far, 2, 6, 1, 7, 0]
    for d in order:
        for j in range(2):
            half[d, j * rank : (j + 1) * rank, :] = (adapter_scale * sums[2 * d + j]).astype(BF)
        if d == far:
            ends = [(half.at[d, :rank], outs[far]), (half.at[d, rank:], outs[-1])]
        else:
            ends = [(half.at[d], outs[d])]
        for source, out in ends:
            stores.append(pltpu.make_async_copy(source, out, out_sems.at[len(stores)]))
            stores[-1].start()
    for store in stores:
        store.wait()


def grad(names, lows, blocks, rank, rows, targets, owned):
    wide = blocks[0].shape[1]
    return pl.pallas_call(
        functools.partial(grad_kernel, rank, rows, len(lows), owned),
        in_specs=smem() + anywhere(len(lows) + len(blocks)),
        out_specs=anywhere(targets + 1),
        out_shape=[
            shape((rank if d in (targets // 2, targets) else 2 * rank, wide))
            for d in range(targets + 1)
        ],
        scratch_shapes=[
            pltpu.VMEM((2 * targets, rank, wide), F32),
            pltpu.VMEM((len(lows),) + lows[0].shape, BF),
            pltpu.VMEM((len(blocks), 2 * rows, wide), BF),
            pltpu.VMEM((targets, 2 * rank, wide), BF),
            pltpu.SemaphoreType.DMA((len(lows) + len(blocks),)),
            pltpu.SemaphoreType.DMA((targets + 1,)),
        ],
        compiler_params=LARGE,
    )(names, *lows, *blocks)


def adam_update(weights, moment, second, gradient):
    moment_new = beta_one * moment + (1.0 - beta_one) * gradient
    second_new = beta_two * second + (1.0 - beta_two) * gradient * gradient
    unbiased_m = moment_new / (1.0 - beta_one**STEP_NUM)
    unbiased_v = second_new / (1.0 - beta_two**STEP_NUM)
    weights_new = weights - step_rate * unbiased_m / (jnp.sqrt(unbiased_v) + adam_eps)
    return (weights_new, moment_new, second_new)


def adam_kernel(parts, *refs):
    grads, refs = refs[:parts], refs[parts:]
    states, outs, refs = refs[:6], refs[6:13], refs[13:]
    here, olds, news, fresh, sems, out_sems = refs[0], refs[1:7], refs[7:13], *refs[13:]
    copies = fetch([*states, *grads], [*olds, *[here.at[d] for d in range(parts)]], sems)
    width = olds[0].shape[1]
    for copy in copies:
        copy.wait()
    total = added([here.at[d] for d in range(parts)])
    for first, cols in ((0, slice(0, width)), (3, slice(width, None))):
        values = adam_update(*[ref[...] for ref in olds[first : first + 3]], total[:, cols])
        for ref, value in zip(news[first : first + 3], values):
            ref[...] = value
        fresh[:, cols] = values[0].astype(BF)
    for store in fetch([*news, fresh], outs, out_sems):
        store.wait()


def adam(grads, state_a, state_b):
    rows, width = state_a[0].shape
    width_b = state_b[0].shape[1]
    wide = width + width_b
    states = [pltpu.VMEM((rows, width), F32)] * 3 + [pltpu.VMEM((rows, width_b), F32)] * 3
    return pl.pallas_call(
        functools.partial(adam_kernel, len(grads)),
        in_specs=anywhere(len(grads) + 6),
        out_specs=anywhere(7),
        out_shape=[shape((rows, width), F32)] * 3
        + [shape((rows, width_b), F32)] * 3
        + [shape((rows, wide))],
        scratch_shapes=[pltpu.VMEM((len(grads), rows, wide), BF)]
        + states
        + states
        + [
            pltpu.VMEM((rows, wide), BF),
            pltpu.SemaphoreType.DMA((len(grads) + 6,)),
            pltpu.SemaphoreType.DMA((7,)),
        ],
        compiler_params=LARGE,
    )(*grads, *state_a, *state_b)


def pick_kernel(rank, index, *refs):
    *refs, out = refs
    for i in range(2):
        device, slot = index[i] // 2, index[i] % 2
        for d, ref in enumerate(refs):

            @pl.when(device == d)
            def _():
                out[i * rank : (i + 1) * rank, :] = block_of(ref, slot, rank)[...]


def pick(index, arrays, rank):
    return pl.pallas_call(
        functools.partial(pick_kernel, rank),
        in_specs=smem(1) + vmem(len(arrays)),
        out_specs=vmem()[0],
        out_shape=shape(arrays[0].shape),
        compiler_params=SMALL,
    )(index, *arrays)


def decode_in_kernel(rank, firsts, parts, slots, *refs):
    xs, refs = refs[:parts], refs[parts:]
    *refs, out = refs
    width = xs[0].shape[1]
    count = xs[0].shape[0]
    for i, x in enumerate(xs):
        here = slots[:, i * count : (i + 1) * count]
        total = jnp.zeros((rank, count), F32)
        for first, ref in zip(firsts, refs):
            both = dot(ref[:, :width], x[...], ((1,), (1,)))
            for j in range(ref.shape[0] // rank):
                total += jnp.where(here == first + j, both[j * rank : (j + 1) * rank], 0.0)
        out[:, i * count : (i + 1) * count] = total


def decode_in(slots, xs, fresh, firsts, rank):
    return pl.pallas_call(
        functools.partial(decode_in_kernel, rank, firsts, len(xs)),
        in_specs=vmem(1 + len(xs) + len(fresh)),
        out_specs=vmem()[0],
        out_shape=shape((rank, slots.shape[1]), F32),
        compiler_params=SMALL,
    )(slots, *xs, *fresh)


def decode_out_kernel(rank, parts, firsts, slots, *refs):
    frozen, refs = refs[:2], refs[2:]
    lows, fresh, out = refs[:parts], refs[parts:-1], refs[-1]
    width_b = out.shape[1]
    total = added(lows).astype(BF).astype(F32)
    result = jnp.concatenate([ref[...] for ref in frozen], axis=0)
    for first, ref in zip(firsts, fresh):
        wide = ref.shape[1]
        both = jnp.concatenate(
            [jnp.where(slots[...] == first + j, total, 0.0) for j in range(ref.shape[0] // rank)],
            axis=0,
        )
        part = dot(both.T.astype(BF), ref[:, wide - width_b :], ((1,), (0,)))
        result += adapter_scale * part
    out[...] = result.astype(BF)


def decode_out(slots, frozen, lows, fresh, firsts, rank):
    return pl.pallas_call(
        functools.partial(decode_out_kernel, rank, len(lows), firsts),
        in_specs=vmem(1 + len(frozen) + len(lows) + len(fresh)),
        out_specs=vmem()[0],
        out_shape=shape((slots.shape[1], frozen[0].shape[1])),
        compiler_params=SMALL,
    )(slots, *frozen, *lows, *fresh)


def add(x, *more):
    total = x.astype(F32)
    for y in more:
        total = total + y.astype(F32)
    return total.astype(x.dtype)


def other_core(x):
    size = lax.axis_size("tensor")
    return lax.ppermute(x, "tensor", [(i, i ^ 1) for i in range(size)])


def chips(x):
    size = lax.axis_size("tensor")
    return [
        lax.ppermute(x, "tensor", [(i, (i + 2 * d) % size) for i in range(size)])
        for d in range(1, size // 2)
    ]


def tensor_parts(x):
    x = add(x, other_core(x))
    return [x, *chips(x)]


def local(
    learn_x,
    learn_dy,
    block_tenant,
    block_count,
    adapter_a,
    adapter_b,
    moment_a,
    moment_b,
    second_a,
    second_b,
    tenant_group,
    decode_inputs,
    dec_weight,
    request_adapter,
):
    groups = lax.axis_size("group")
    rows_dp = lax.axis_size("dp")
    group = lax.axis_index("group")
    row = lax.axis_index("dp")
    owned, rank, width = adapter_a.shape
    width_b = adapter_b.shape[2]
    span = groups * owned
    barrier = lax.optimization_barrier

    def flat(x):
        return x.reshape(owned * rank, x.shape[2])

    blocks = block_tenant.shape[0]
    rows = learn_x.shape[0] // blocks
    packed = begin(block_tenant, block_count, learn_x, learn_dy, groups)
    packed, state = barrier((packed, (adapter_a, adapter_b)))
    order = sorted(range(1, groups), key=lambda d: min(d, groups - d))
    moved = {d: shift(packed[d], "group", d) for d in order}
    arrived = [packed[0]] + [moved[d] for d in range(1, groups)]
    own = jnp.concatenate([flat(x).astype(BF) for x in state], axis=1)
    tables, firsts = ring(own, rows_dp, owned)
    requests = decode_inputs[0]
    steps = requests.shape[1]
    tensor = lax.axis_index("tensor").reshape(1)
    tables, requests = barrier((tables, requests))
    early = frozen(tensor, requests, dec_weight, 0, 2, width, LARGE)
    arrived, tables, early = barrier((arrived, tables, early))

    mine, his, names = low(tables, firsts, arrived, rank, rows, rows_dp, owned)
    mine = add(mine, other_core(his))
    mine = add(mine, *chips(mine))
    lows = [mine, other_core(mine)]
    sums = grad(names, lows, arrived, rank, rows, rows_dp, owned)
    pieces = [sums[0], *two_stage_reduce(sums, rows_dp)]
    *new, fresh = adam(
        pieces,
        [flat(x) for x in (adapter_a, moment_a, second_a)],
        [flat(x) for x in (adapter_b, moment_b, second_b)],
    )

    tenant_ids = jnp.arange(tenant_group.shape[0], dtype=jnp.int32)
    served = (tenant_group == group).astype(jnp.int32)
    by_row = served.reshape(rows_dp, span)
    slot_of = jnp.cumsum(by_row, axis=1) - by_row
    mine = lax.dynamic_slice_in_dim(by_row, row, 1, 0)[0]
    mine_slot = lax.dynamic_slice_in_dim(slot_of, row, 1, 0)[0]
    position = jnp.arange(span, dtype=jnp.int32)
    relative = ((group - position // owned) % groups) * owned + position % owned
    wanted = jnp.sum(
        jnp.where(
            (mine[None, :] == 1)
            & (mine_slot[None, :] == jnp.arange(owned, dtype=jnp.int32)[:, None]),
            relative[None, :],
            0,
        ),
        axis=1,
        dtype=jnp.int32,
    )
    slot_here = ((row - tenant_ids // span) % rows_dp) * owned + slot_of.reshape(-1)
    slot_here = jnp.where(served == 1, slot_here, -1)
    request_slot = jnp.sum(
        jnp.where(request_adapter[0][:, None] == tenant_ids[None, :], slot_here[None, :], 0),
        axis=1,
        dtype=jnp.int32,
    )
    count = requests.shape[0] * steps
    slots = jnp.broadcast_to(request_slot[:, None], (requests.shape[0], steps)).reshape(1, count)
    *new, fresh = adam(
        pieces,
        [flat(x) for x in (adapter_a, moment_a, second_a)],
        [flat(x) for x in (adapter_b, moment_b, second_b)],
    )
    in_row = spread(fresh, "group")
    fresh, wanted, slots, requests = barrier((fresh, wanted, slots, requests))
    late = frozen(tensor, requests, dec_weight, 1, 2, width, MIDDLE)
    in_row, wanted, slots, late = barrier((in_row, wanted, slots, late))
    served_fresh, firsts = two_stage(pick(wanted, in_row, rank), rows_dp, owned)

    dec_part = decode_in(slots, [early[1], late[1]], served_fresh, firsts, rank)
    decoded = decode_out(
        slots, [early[0], late[0]], tensor_parts(dec_part), served_fresh, firsts, rank
    )
    new_a = [x.reshape(adapter_a.shape) for x in new[:3]]
    new_b = [x.reshape(adapter_b.shape) for x in new[3:]]
    return (
        new_a[0],
        new_b[0],
        new_a[1],
        new_b[1],
        new_a[2],
        new_b[2],
        decoded.reshape((1,) + requests.shape[:2] + (width_b,)),
    )


def solution(mesh):
    state = P(("dp", "group"), None, "tensor")
    return jax.shard_map(
        local,
        mesh=mesh,
        in_specs=(
            P(("dp", "group"), "tensor"),
            P(("dp", "group"), "tensor"),
            P(("dp", "group")),
            P(("dp", "group")),
            state,
            state,
            state,
            state,
            state,
            state,
            P(),
            P("group", "dp", None, None),
            P(None, "tensor"),
            P("group", "dp"),
        ),
        out_specs=(
            state,
            state,
            state,
            state,
            state,
            state,
            P("group", "dp", None, "tensor"),
        ),
        check_vma=False,
    )
```

```python
import functools

import jax
import jax.numpy as jnp
from jax import lax
from jax.experimental import pallas as pl
from jax.experimental.pallas import tpu as pltpu
from jax.sharding import PartitionSpec as P

STEP_NUM = 10

adapter_scale = 2.0
beta_one = 0.9
beta_two = 0.999
step_rate = 0.001
adam_eps = 1e-08

BF = jnp.bfloat16
F32 = jnp.float32
MIB = 1024 * 1024


def dot(a, b, dims):
    return lax.dot_general(a, b, (dims, ((), ())), preferred_element_type=F32)


def shift(x, axis, distance):
    size = lax.axis_size(axis)
    return lax.ppermute(x, axis, [(i, (i + distance) % size) for i in range(size)])


def spread(x, axis):
    return [x] + [shift(x, axis, d) for d in range(1, lax.axis_size(axis))]


def ring(x, size, owned):
    ahead = behind = x
    arrays, firsts = [x], [0]
    for hop in range(1, size // 2 + 1):
        ahead = shift(ahead, "dp", 1)
        arrays.append(ahead)
        firsts.append(hop * owned)
        if hop < size // 2:
            behind = shift(behind, "dp", -1)
            arrays.append(behind)
            firsts.append((size - hop) * owned)
    return arrays, firsts


def two_stage(x, size, owned):
    near = [shift(x, "dp", d) for d in (1, -1, 2, -2)]
    far = [shift(near[2], "dp", 1), shift(near[3], "dp", -1), shift(near[2], "dp", 2)]
    firsts = [d % size * owned for d in (0, 1, -1, 2, -2, 3, -3, 4)]
    return [x, *near, *far], firsts


def two_stage_reduce(x, size):
    upper, lower = x[size // 2], x[-1]
    half = upper.shape[0]
    after, before = shift(x[3], "dp", 1), shift(x[5], "dp", -1)
    far_after, far_before = shift(upper, "dp", 2), shift(lower, "dp", -2)
    after, before, one, other = lax.optimization_barrier((after, before, x[1], x[7]))
    near = [shift(one, "dp", 1), shift(other, "dp", -1)]
    ahead = jnp.concatenate(
        [add(x[2][:half], after[:half], far_after), add(x[2][half:], after[half:])]
    )
    behind = jnp.concatenate(
        [add(x[6][:half], before[:half]), add(x[6][half:], before[half:], far_before)]
    )
    return [*near, shift(ahead, "dp", 2), shift(behind, "dp", -2)]


def spot(memory, n=1):
    return [pl.BlockSpec(memory_space=memory)] * n


vmem = functools.partial(spot, pltpu.VMEM)
smem = functools.partial(spot, pltpu.SMEM)
anywhere = functools.partial(spot, pl.ANY)
SMALL = pltpu.CompilerParams(vmem_limit_bytes=14 * MIB)
MIDDLE = pltpu.CompilerParams(vmem_limit_bytes=52 * MIB)
WHOLE = pltpu.CompilerParams(vmem_limit_bytes=64 * MIB)
LARGE = pltpu.CompilerParams(vmem_limit_bytes=61 * MIB)


def shape(dims, dtype=BF):
    return jax.ShapeDtypeStruct(dims, dtype)


def block_of(ref, index, rows):
    return ref.at[pl.ds(pl.multiple_of(index * rows, rows), rows), :]


def fetch(refs, rooms, sems):
    copies = [
        pltpu.make_async_copy(ref, room, sems.at[i]) for i, (ref, room) in enumerate(zip(refs, rooms))
    ]
    for copy in copies:
        copy.start()
    return copies


def begin_kernel(rows, groups, tenant, count, x, dy, *refs):
    packs, refs = refs[:groups], refs[groups:]
    source, ids, dy_here, room, sems, x_sems, out_sems = refs
    blocks = 2 * groups
    width = x.shape[1]
    loads = fetch([dy], [dy_here], sems)
    group = lax.axis_index("group")
    names = [tenant[b] for b in range(blocks)]
    far = [lax.rem(lax.rem(name // 2, groups) - group + groups, groups) for name in names]
    for b in range(blocks):
        place = 2 * far[b]
        for e in range(b):
            place += (far[e] == far[b]).astype(jnp.int32)
        source[place] = b
        ids[place] = names[b]
    moves = []
    for s in range(blocks):
        part = pl.ds((s % 2) * rows, rows)
        moves.append(
            pltpu.make_async_copy(
                block_of(x, source[s], rows), room.at[s // 2, part, :width], x_sems.at[s]
            )
        )
        moves[-1].start()
    loads[0].wait()
    for s in range(blocks):
        block = block_of(dy_here, source[s], rows)[...].astype(F32)
        live = lax.broadcasted_iota(jnp.int32, block.shape, 0) < count[source[s]]
        block = jnp.where(live, block, 0.0).astype(BF)
        room[s // 2, (s % 2) * rows : (s % 2 + 1) * rows, width:] = block
    stores = []
    for d in range(groups):
        lane = lax.broadcasted_iota(jnp.int32, (16, dy.shape[1]), 1)
        both = jnp.where(lane == 0, ids[2 * d], ids[2 * d + 1])
        room[d, 2 * rows :, width:] = both.astype(F32).astype(BF)
        room[d, 2 * rows :, :width] = jnp.zeros((16, width), BF)
        moves[2 * d].wait()
        moves[2 * d + 1].wait()
        stores.append(pltpu.make_async_copy(room.at[d], packs[d], out_sems.at[d]))
        stores[-1].start()
    for store in stores:
        store.wait()


def begin(tenant, count, x, dy, groups):
    rows = x.shape[0] // tenant.shape[0]
    wide = x.shape[1] + dy.shape[1]
    return pl.pallas_call(
        functools.partial(begin_kernel, rows, groups),
        in_specs=smem(2) + anywhere(2),
        out_specs=anywhere(groups),
        out_shape=[shape((2 * rows + 16, wide))] * groups,
        scratch_shapes=[
            pltpu.SMEM((2 * groups,), jnp.int32),
            pltpu.SMEM((2 * groups,), jnp.int32),
            pltpu.VMEM(dy.shape, BF),
            pltpu.VMEM((groups, 2 * rows + 16, wide), BF),
            pltpu.SemaphoreType.DMA((1,)),
            pltpu.SemaphoreType.DMA((2 * groups,)),
            pltpu.SemaphoreType.DMA((groups,)),
        ],
        compiler_params=LARGE,
    )(tenant, count, x, dy)


def frozen_kernel(tensor, x, weight, out, x_out):
    step = pl.program_id(0)
    width = x_out.shape[1]
    pieces = x.shape[2] // width
    block = x[...].reshape(out.shape[0], x.shape[2])

    @pl.when(step == 0)
    def _():
        out[...] = jnp.zeros_like(out)

    out[...] += dot(block, weight[...], ((1,), (0,)))
    for i in range(pieces):

        @pl.when(tensor[0] == step * pieces + i)
        def _():
            x_out[...] = block[:, i * width : (i + 1) * width]


def frozen(tensor, requests, weight, part, parts, width, params):
    count = requests.shape[0] // parts
    steps = requests.shape[1]
    width_b = weight.shape[1]
    wide = 4 * width
    return pl.pallas_call(
        frozen_kernel,
        grid_spec=pltpu.PrefetchScalarGridSpec(
            num_scalar_prefetch=1,
            grid=(requests.shape[2] // wide,),
            in_specs=[
                pl.BlockSpec((count, steps, wide), lambda k, tensor: (part, 0, k)),
                pl.BlockSpec((wide, width_b), lambda k, tensor: (k, 0)),
            ],
            out_specs=[
                pl.BlockSpec((count * steps, width_b), lambda k, tensor: (0, 0)),
                pl.BlockSpec((count * steps, width), lambda k, tensor: (0, 0)),
            ],
        ),
        out_shape=[shape((count * steps, width_b), F32), shape((count * steps, width))],
        compiler_params=params,
    )(tensor, requests, weight)


def low_kernel(rank, rows, size, owned, firsts, *refs):
    parts = len(firsts)
    tables, refs = refs[:parts], refs[parts:]
    *blocks, mine, his, names, table, here, both, sems = refs
    core = lax.rem(lax.axis_index("tensor"), 2)
    wide = table.shape[1]
    width = wide - 128
    row = lax.axis_index("dp")
    span = owned * len(blocks)
    used = 2 * rows
    rooms = [
        table.at[first * rank : first * rank + ref.shape[0], :] for first, ref in zip(firsts, tables)
    ]
    rooms += [here.at[d] for d in range(len(blocks))]
    copies = fetch([*tables, *blocks], rooms, sems)
    for copy in copies[:parts]:
        copy.wait()
    for s in range(2 * len(blocks)):
        if s % 2 == 0:
            copies[parts + s // 2].wait()
            ids = here[s // 2, used : used + 16, width:].astype(F32)
        name = ids[0, s % 2].astype(jnp.int32)
        place = lax.rem(row - name // span + size, size) * owned + lax.rem(name, owned)
        names[s] = name
        block = here[s // 2, (s % 2) * rows : (s % 2 + 1) * rows, :]
        chosen = block_of(table, place, rank)[...]
        low_in = dot(chosen[:, :width], block[:, :width], ((1,), (1,)))
        low_back = dot(chosen[:, width:], block[:, width:], ((1,), (1,)))
        both[0, s * rank : (s + 1) * rank, :] = low_in.astype(BF)
        both[1, s * rank : (s + 1) * rank, :] = low_back.astype(BF)
    mine[...] = both[core]
    his[...] = both[1 - core]


def low(tables, firsts, blocks, rank, rows, size, owned):
    wide = blocks[0].shape[1]
    total = sum(table.shape[0] for table in tables)
    return pl.pallas_call(
        functools.partial(low_kernel, rank, rows, size, owned, firsts),
        in_specs=anywhere(len(tables) + len(blocks)),
        out_specs=vmem(2) + smem(),
        out_shape=[
            shape((2 * len(blocks) * rank, rows)),
            shape((2 * len(blocks) * rank, rows)),
            shape((2 * len(blocks),), jnp.int32),
        ],
        scratch_shapes=[
            pltpu.VMEM((total, wide), BF),
            pltpu.VMEM((len(blocks),) + blocks[0].shape, BF),
            pltpu.VMEM((2, 2 * len(blocks) * rank, rows), BF),
            pltpu.SemaphoreType.DMA((len(tables) + len(blocks),)),
        ],
        compiler_params=LARGE,
    )(*tables, *blocks)


def added(refs):
    total = refs[0][...].astype(F32)
    for ref in refs[1:]:
        total = total + ref[...].astype(F32)
    return total


def grad_kernel(rank, rows, parts, owned, names, *refs):
    lows, refs = refs[:parts], refs[parts:]
    groups = lows[0].shape[0] // (2 * rank)
    core = lax.rem(lax.axis_index("tensor"), 2)
    blocks, refs = refs[:groups], refs[groups:]
    *outs, sums, lows_here, here, half, sems, out_sems = refs
    width = sums.shape[2] - 128
    row = lax.axis_index("dp")
    span, size = owned * groups, len(outs) - 1
    copies = fetch(
        [*lows, *[ref.at[: 2 * rows, :] for ref in blocks]],
        [*[lows_here.at[d] for d in range(parts)], *[here.at[d] for d in range(groups)]],
        sems,
    )
    sums[...] = jnp.zeros_like(sums)
    for copy in copies[:parts]:
        copy.wait()
    for s in range(2 * groups):
        if s % 2 == 0:
            copies[parts + s // 2].wait()
        block = here[s // 2, (s % 2) * rows : (s % 2 + 1) * rows, :]
        low_in = lows_here[core, s * rank : (s + 1) * rank, :]
        low_back = lows_here[1 - core, s * rank : (s + 1) * rank, :]
        name = names[s]
        place = lax.rem(name // span - row + size, size) * owned + lax.rem(name, owned)
        sums[place, :, :width] += dot(low_back, block[:, :width], ((1,), (0,)))
        sums[place, :, width:] += dot(low_in, block[:, width:], ((1,), (0,)))
    stores = []
    far = size // 2
    order = [3, 5, far, 2, 6, 1, 7, 0]
    for d in order:
        for j in range(2):
            half[d, j * rank : (j + 1) * rank, :] = (adapter_scale * sums[2 * d + j]).astype(BF)
        if d == far:
            ends = [(half.at[d, :rank], outs[far]), (half.at[d, rank:], outs[-1])]
        else:
            ends = [(half.at[d], outs[d])]
        for source, out in ends:
            stores.append(pltpu.make_async_copy(source, out, out_sems.at[len(stores)]))
            stores[-1].start()
    for store in stores:
        store.wait()


def grad(names, lows, blocks, rank, rows, targets, owned):
    wide = blocks[0].shape[1]
    return pl.pallas_call(
        functools.partial(grad_kernel, rank, rows, len(lows), owned),
        in_specs=smem() + anywhere(len(lows) + len(blocks)),
        out_specs=anywhere(targets + 1),
        out_shape=[
            shape((rank if d in (targets // 2, targets) else 2 * rank, wide))
            for d in range(targets + 1)
        ],
        scratch_shapes=[
            pltpu.VMEM((2 * targets, rank, wide), F32),
            pltpu.VMEM((len(lows),) + lows[0].shape, BF),
            pltpu.VMEM((len(blocks), 2 * rows, wide), BF),
            pltpu.VMEM((targets, 2 * rank, wide), BF),
            pltpu.SemaphoreType.DMA((len(lows) + len(blocks),)),
            pltpu.SemaphoreType.DMA((targets + 1,)),
        ],
        compiler_params=LARGE,
    )(names, *lows, *blocks)


def adam_update(weights, moment, second, gradient):
    moment_new = beta_one * moment + (1.0 - beta_one) * gradient
    second_new = beta_two * second + (1.0 - beta_two) * gradient * gradient
    unbiased_m = moment_new / (1.0 - beta_one**STEP_NUM)
    unbiased_v = second_new / (1.0 - beta_two**STEP_NUM)
    weights_new = weights - step_rate * unbiased_m / (jnp.sqrt(unbiased_v) + adam_eps)
    return (weights_new, moment_new, second_new)


def adam_kernel(parts, *refs):
    grads, refs = refs[:parts], refs[parts:]
    states, outs, refs = refs[:6], refs[6:13], refs[13:]
    here, olds, news, fresh, sems, out_sems = refs[0], refs[1:7], refs[7:13], *refs[13:]
    copies = fetch([*states, *grads], [*olds, *[here.at[d] for d in range(parts)]], sems)
    width = olds[0].shape[1]
    for copy in copies:
        copy.wait()
    total = added([here.at[d] for d in range(parts)])
    for first, cols in ((0, slice(0, width)), (3, slice(width, None))):
        values = adam_update(*[ref[...] for ref in olds[first : first + 3]], total[:, cols])
        for ref, value in zip(news[first : first + 3], values):
            ref[...] = value
        fresh[:, cols] = values[0].astype(BF)
    for store in fetch([*news, fresh], outs, out_sems):
        store.wait()


def adam(grads, state_a, state_b):
    rows, width = state_a[0].shape
    width_b = state_b[0].shape[1]
    wide = width + width_b
    states = [pltpu.VMEM((rows, width), F32)] * 3 + [pltpu.VMEM((rows, width_b), F32)] * 3
    return pl.pallas_call(
        functools.partial(adam_kernel, len(grads)),
        in_specs=anywhere(len(grads) + 6),
        out_specs=anywhere(7),
        out_shape=[shape((rows, width), F32)] * 3
        + [shape((rows, width_b), F32)] * 3
        + [shape((rows, wide))],
        scratch_shapes=[pltpu.VMEM((len(grads), rows, wide), BF)]
        + states
        + states
        + [
            pltpu.VMEM((rows, wide), BF),
            pltpu.SemaphoreType.DMA((len(grads) + 6,)),
            pltpu.SemaphoreType.DMA((7,)),
        ],
        compiler_params=LARGE,
    )(*grads, *state_a, *state_b)


def pick_kernel(rank, index, *refs):
    *refs, out = refs
    for i in range(2):
        device, slot = index[i] // 2, index[i] % 2
        for d, ref in enumerate(refs):

            @pl.when(device == d)
            def _():
                out[i * rank : (i + 1) * rank, :] = block_of(ref, slot, rank)[...]


def pick(index, arrays, rank):
    return pl.pallas_call(
        functools.partial(pick_kernel, rank),
        in_specs=smem(1) + vmem(len(arrays)),
        out_specs=vmem()[0],
        out_shape=shape(arrays[0].shape),
        compiler_params=SMALL,
    )(index, *arrays)


def decode_in_kernel(rank, firsts, parts, slots, *refs):
    xs, refs = refs[:parts], refs[parts:]
    *refs, out = refs
    width = xs[0].shape[1]
    count = xs[0].shape[0]
    for i, x in enumerate(xs):
        here = slots[:, i * count : (i + 1) * count]
        total = jnp.zeros((rank, count), F32)
        for first, ref in zip(firsts, refs):
            both = dot(ref[:, :width], x[...], ((1,), (1,)))
            for j in range(ref.shape[0] // rank):
                total += jnp.where(here == first + j, both[j * rank : (j + 1) * rank], 0.0)
        out[:, i * count : (i + 1) * count] = total


def decode_in(slots, xs, fresh, firsts, rank):
    return pl.pallas_call(
        functools.partial(decode_in_kernel, rank, firsts, len(xs)),
        in_specs=vmem(1 + len(xs) + len(fresh)),
        out_specs=vmem()[0],
        out_shape=shape((rank, slots.shape[1]), F32),
        compiler_params=SMALL,
    )(slots, *xs, *fresh)


def decode_out_kernel(rank, parts, firsts, slots, *refs):
    frozen, refs = refs[:2], refs[2:]
    lows, fresh, out = refs[:parts], refs[parts:-1], refs[-1]
    width_b = out.shape[1]
    total = added(lows).astype(BF).astype(F32)
    result = jnp.concatenate([ref[...] for ref in frozen], axis=0)
    for first, ref in zip(firsts, fresh):
        wide = ref.shape[1]
        both = jnp.concatenate(
            [jnp.where(slots[...] == first + j, total, 0.0) for j in range(ref.shape[0] // rank)],
            axis=0,
        )
        part = dot(both.T.astype(BF), ref[:, wide - width_b :], ((1,), (0,)))
        result += adapter_scale * part
    out[...] = result.astype(BF)


def decode_out(slots, frozen, lows, fresh, firsts, rank):
    return pl.pallas_call(
        functools.partial(decode_out_kernel, rank, len(lows), firsts),
        in_specs=vmem(1 + len(frozen) + len(lows) + len(fresh)),
        out_specs=vmem()[0],
        out_shape=shape((slots.shape[1], frozen[0].shape[1])),
        compiler_params=SMALL,
    )(slots, *frozen, *lows, *fresh)


def add(x, *more):
    total = x.astype(F32)
    for y in more:
        total = total + y.astype(F32)
    return total.astype(x.dtype)


def other_core(x):
    size = lax.axis_size("tensor")
    return lax.ppermute(x, "tensor", [(i, i ^ 1) for i in range(size)])


def chips(x):
    size = lax.axis_size("tensor")
    return [
        lax.ppermute(x, "tensor", [(i, (i + 2 * d) % size) for i in range(size)])
        for d in range(1, size // 2)
    ]


def tensor_parts(x):
    x = add(x, other_core(x))
    return [x, *chips(x)]


def local(
    learn_x,
    learn_dy,
    block_tenant,
    block_count,
    adapter_a,
    adapter_b,
    moment_a,
    moment_b,
    second_a,
    second_b,
    tenant_group,
    decode_inputs,
    dec_weight,
    request_adapter,
):
    groups = lax.axis_size("group")
    rows_dp = lax.axis_size("dp")
    group = lax.axis_index("group")
    row = lax.axis_index("dp")
    owned, rank, width = adapter_a.shape
    width_b = adapter_b.shape[2]
    span = groups * owned
    barrier = lax.optimization_barrier

    def flat(x):
        return x.reshape(owned * rank, x.shape[2])

    blocks = block_tenant.shape[0]
    rows = learn_x.shape[0] // blocks
    packed = begin(block_tenant, block_count, learn_x, learn_dy, groups)
    packed, state = barrier((packed, (adapter_a, adapter_b)))
    order = sorted(range(1, groups), key=lambda d: min(d, groups - d))
    moved = {d: shift(packed[d], "group", d) for d in order}
    arrived = [packed[0]] + [moved[d] for d in range(1, groups)]
    own = jnp.concatenate([flat(x).astype(BF) for x in state], axis=1)
    tables, firsts = ring(own, rows_dp, owned)
    requests = decode_inputs[0]
    steps = requests.shape[1]
    tensor = lax.axis_index("tensor").reshape(1)
    tables, requests = barrier((tables, requests))
    early = frozen(tensor, requests, dec_weight, 0, 2, width, WHOLE)
    arrived, tables, early = barrier((arrived, tables, early))

    mine, his, names = low(tables, firsts, arrived, rank, rows, rows_dp, owned)
    mine = add(mine, other_core(his))
    mine = add(mine, *chips(mine))
    lows = [mine, other_core(mine)]
    sums = grad(names, lows, arrived, rank, rows, rows_dp, owned)
    pieces = [sums[0], *two_stage_reduce(sums, rows_dp)]
    *new, fresh = adam(
        pieces,
        [flat(x) for x in (adapter_a, moment_a, second_a)],
        [flat(x) for x in (adapter_b, moment_b, second_b)],
    )

    tenant_ids = jnp.arange(tenant_group.shape[0], dtype=jnp.int32)
    served = (tenant_group == group).astype(jnp.int32)
    by_row = served.reshape(rows_dp, span)
    slot_of = jnp.cumsum(by_row, axis=1) - by_row
    mine = lax.dynamic_slice_in_dim(by_row, row, 1, 0)[0]
    mine_slot = lax.dynamic_slice_in_dim(slot_of, row, 1, 0)[0]
    position = jnp.arange(span, dtype=jnp.int32)
    relative = ((group - position // owned) % groups) * owned + position % owned
    wanted = jnp.sum(
        jnp.where(
            (mine[None, :] == 1)
            & (mine_slot[None, :] == jnp.arange(owned, dtype=jnp.int32)[:, None]),
            relative[None, :],
            0,
        ),
        axis=1,
        dtype=jnp.int32,
    )
    slot_here = ((row - tenant_ids // span) % rows_dp) * owned + slot_of.reshape(-1)
    slot_here = jnp.where(served == 1, slot_here, -1)
    request_slot = jnp.sum(
        jnp.where(request_adapter[0][:, None] == tenant_ids[None, :], slot_here[None, :], 0),
        axis=1,
        dtype=jnp.int32,
    )
    count = requests.shape[0] * steps
    slots = jnp.broadcast_to(request_slot[:, None], (requests.shape[0], steps)).reshape(1, count)
    *new, fresh = adam(
        pieces,
        [flat(x) for x in (adapter_a, moment_a, second_a)],
        [flat(x) for x in (adapter_b, moment_b, second_b)],
    )
    in_row = spread(fresh, "group")
    fresh, wanted, slots, requests = barrier((fresh, wanted, slots, requests))
    late = frozen(tensor, requests, dec_weight, 1, 2, width, MIDDLE)
    in_row, wanted, slots, late = barrier((in_row, wanted, slots, late))
    served_fresh, firsts = two_stage(pick(wanted, in_row, rank), rows_dp, owned)

    dec_part = decode_in(slots, [early[1], late[1]], served_fresh, firsts, rank)
    decoded = decode_out(
        slots, [early[0], late[0]], tensor_parts(dec_part), served_fresh, firsts, rank
    )
    new_a = [x.reshape(adapter_a.shape) for x in new[:3]]
    new_b = [x.reshape(adapter_b.shape) for x in new[3:]]
    return (
        new_a[0],
        new_b[0],
        new_a[1],
        new_b[1],
        new_a[2],
        new_b[2],
        decoded.reshape((1,) + requests.shape[:2] + (width_b,)),
    )


def solution(mesh):
    state = P(("dp", "group"), None, "tensor")
    return jax.shard_map(
        local,
        mesh=mesh,
        in_specs=(
            P(("dp", "group"), "tensor"),
            P(("dp", "group"), "tensor"),
            P(("dp", "group")),
            P(("dp", "group")),
            state,
            state,
            state,
            state,
            state,
            state,
            P(),
            P("group", "dp", None, None),
            P(None, "tensor"),
            P("group", "dp"),
        ),
        out_specs=(
            state,
            state,
            state,
            state,
            state,
            state,
            P("group", "dp", None, "tensor"),
        ),
        check_vma=False,
    )
```

```python
import functools

import jax
import jax.numpy as jnp
from jax import lax
from jax.experimental import pallas as pl
from jax.experimental.pallas import tpu as pltpu
from jax.sharding import PartitionSpec as P

STEP_NUM = 10

adapter_scale = 2.0
beta_one = 0.9
beta_two = 0.999
step_rate = 0.001
adam_eps = 1e-08

BF = jnp.bfloat16
F32 = jnp.float32
MIB = 1024 * 1024


def dot(a, b, dims):
    return lax.dot_general(a, b, (dims, ((), ())), preferred_element_type=F32)


def shift(x, axis, distance):
    size = lax.axis_size(axis)
    return lax.ppermute(x, axis, [(i, (i + distance) % size) for i in range(size)])


def spread(x, axis):
    return [x] + [shift(x, axis, d) for d in range(1, lax.axis_size(axis))]


def ring(x, size, owned):
    ahead = behind = x
    arrays, firsts = [x], [0]
    for hop in range(1, size // 2 + 1):
        ahead = shift(ahead, "dp", 1)
        arrays.append(ahead)
        firsts.append(hop * owned)
        if hop < size // 2:
            behind = shift(behind, "dp", -1)
            arrays.append(behind)
            firsts.append((size - hop) * owned)
    return arrays, firsts


def two_stage(x, size, owned):
    near = [shift(x, "dp", d) for d in (1, -1, 2, -2)]
    far = [shift(near[2], "dp", 1), shift(near[3], "dp", -1), shift(near[2], "dp", 2)]
    firsts = [d % size * owned for d in (0, 1, -1, 2, -2, 3, -3, 4)]
    return [x, *near, *far], firsts


def two_stage_reduce(x, size):
    upper, lower = x[size // 2], x[-1]
    half = upper.shape[0]
    after, before = shift(x[3], "dp", 1), shift(x[5], "dp", -1)
    far_after, far_before = shift(upper, "dp", 2), shift(lower, "dp", -2)
    after, before, one, other = lax.optimization_barrier((after, before, x[1], x[7]))
    near = [shift(one, "dp", 1), shift(other, "dp", -1)]
    ahead = jnp.concatenate(
        [add(x[2][:half], after[:half], far_after), add(x[2][half:], after[half:])]
    )
    behind = jnp.concatenate(
        [add(x[6][:half], before[:half]), add(x[6][half:], before[half:], far_before)]
    )
    return [*near, shift(ahead, "dp", 2), shift(behind, "dp", -2)]


def spot(memory, n=1):
    return [pl.BlockSpec(memory_space=memory)] * n


vmem = functools.partial(spot, pltpu.VMEM)
smem = functools.partial(spot, pltpu.SMEM)
anywhere = functools.partial(spot, pl.ANY)
SMALL = pltpu.CompilerParams(vmem_limit_bytes=14 * MIB)
MIDDLE = pltpu.CompilerParams(vmem_limit_bytes=52 * MIB)
WHOLE = pltpu.CompilerParams(vmem_limit_bytes=64 * MIB)
LARGE = pltpu.CompilerParams(vmem_limit_bytes=61 * MIB)


def shape(dims, dtype=BF):
    return jax.ShapeDtypeStruct(dims, dtype)


def block_of(ref, index, rows):
    return ref.at[pl.ds(pl.multiple_of(index * rows, rows), rows), :]


def fetch(refs, rooms, sems):
    copies = [
        pltpu.make_async_copy(ref, room, sems.at[i]) for i, (ref, room) in enumerate(zip(refs, rooms))
    ]
    for copy in copies:
        copy.start()
    return copies


def begin_kernel(rows, groups, tenant, count, x, dy, *refs):
    packs, refs = refs[:groups], refs[groups:]
    source, ids, dy_here, room, sems, x_sems, out_sems = refs
    blocks = 2 * groups
    width = x.shape[1]
    loads = fetch([dy], [dy_here], sems)
    group = lax.axis_index("group")
    names = [tenant[b] for b in range(blocks)]
    far = [lax.rem(lax.rem(name // 2, groups) - group + groups, groups) for name in names]
    for b in range(blocks):
        place = 2 * far[b]
        for e in range(b):
            place += (far[e] == far[b]).astype(jnp.int32)
        source[place] = b
        ids[place] = names[b]
    moves = []
    for s in range(blocks):
        part = pl.ds((s % 2) * rows, rows)
        moves.append(
            pltpu.make_async_copy(
                block_of(x, source[s], rows), room.at[s // 2, part, :width], x_sems.at[s]
            )
        )
        moves[-1].start()
    loads[0].wait()
    for s in range(blocks):
        block = block_of(dy_here, source[s], rows)[...].astype(F32)
        live = lax.broadcasted_iota(jnp.int32, block.shape, 0) < count[source[s]]
        block = jnp.where(live, block, 0.0).astype(BF)
        room[s // 2, (s % 2) * rows : (s % 2 + 1) * rows, width:] = block
    stores = []
    for d in range(groups):
        lane = lax.broadcasted_iota(jnp.int32, (16, dy.shape[1]), 1)
        both = jnp.where(lane == 0, ids[2 * d], ids[2 * d + 1])
        room[d, 2 * rows :, width:] = both.astype(F32).astype(BF)
        room[d, 2 * rows :, :width] = jnp.zeros((16, width), BF)
        moves[2 * d].wait()
        moves[2 * d + 1].wait()
        stores.append(pltpu.make_async_copy(room.at[d], packs[d], out_sems.at[d]))
        stores[-1].start()
    for store in stores:
        store.wait()


def begin(tenant, count, x, dy, groups):
    rows = x.shape[0] // tenant.shape[0]
    wide = x.shape[1] + dy.shape[1]
    return pl.pallas_call(
        functools.partial(begin_kernel, rows, groups),
        in_specs=smem(2) + anywhere(2),
        out_specs=anywhere(groups),
        out_shape=[shape((2 * rows + 16, wide))] * groups,
        scratch_shapes=[
            pltpu.SMEM((2 * groups,), jnp.int32),
            pltpu.SMEM((2 * groups,), jnp.int32),
            pltpu.VMEM(dy.shape, BF),
            pltpu.VMEM((groups, 2 * rows + 16, wide), BF),
            pltpu.SemaphoreType.DMA((1,)),
            pltpu.SemaphoreType.DMA((2 * groups,)),
            pltpu.SemaphoreType.DMA((groups,)),
        ],
        compiler_params=LARGE,
    )(tenant, count, x, dy)


def frozen_kernel(tensor, x, weight, out, x_out):
    step = pl.program_id(0)
    width = x_out.shape[1]
    pieces = x.shape[2] // width
    block = x[...].reshape(out.shape[0], x.shape[2])

    @pl.when(step == 0)
    def _():
        out[...] = jnp.zeros_like(out)

    out[...] += dot(block, weight[...], ((1,), (0,)))
    for i in range(pieces):

        @pl.when(tensor[0] == step * pieces + i)
        def _():
            x_out[...] = block[:, i * width : (i + 1) * width]


def frozen(tensor, requests, weight, part, parts, width, params):
    count = requests.shape[0] // parts
    steps = requests.shape[1]
    width_b = weight.shape[1]
    wide = 4 * width
    return pl.pallas_call(
        frozen_kernel,
        grid_spec=pltpu.PrefetchScalarGridSpec(
            num_scalar_prefetch=1,
            grid=(requests.shape[2] // wide,),
            in_specs=[
                pl.BlockSpec((count, steps, wide), lambda k, tensor: (part, 0, k)),
                pl.BlockSpec((wide, width_b), lambda k, tensor: (k, 0)),
            ],
            out_specs=[
                pl.BlockSpec((count * steps, width_b), lambda k, tensor: (0, 0)),
                pl.BlockSpec((count * steps, width), lambda k, tensor: (0, 0)),
            ],
        ),
        out_shape=[shape((count * steps, width_b), F32), shape((count * steps, width))],
        compiler_params=params,
    )(tensor, requests, weight)


def low_kernel(rank, rows, size, owned, firsts, *refs):
    parts = len(firsts)
    tables, refs = refs[:parts], refs[parts:]
    *blocks, mine, his, names, table, here, both, sems = refs
    core = lax.rem(lax.axis_index("tensor"), 2)
    wide = table.shape[1]
    width = wide - 128
    row = lax.axis_index("dp")
    span = owned * len(blocks)
    used = 2 * rows
    rooms = [
        table.at[first * rank : first * rank + ref.shape[0], :] for first, ref in zip(firsts, tables)
    ]
    rooms += [here.at[d] for d in range(len(blocks))]
    copies = fetch([*tables, *blocks], rooms, sems)
    for copy in copies[:parts]:
        copy.wait()
    for s in range(2 * len(blocks)):
        if s % 2 == 0:
            copies[parts + s // 2].wait()
            ids = here[s // 2, used : used + 16, width:].astype(F32)
        name = ids[0, s % 2].astype(jnp.int32)
        place = lax.rem(row - name // span + size, size) * owned + lax.rem(name, owned)
        names[s] = name
        block = here[s // 2, (s % 2) * rows : (s % 2 + 1) * rows, :]
        chosen = block_of(table, place, rank)[...]
        low_in = dot(chosen[:, :width], block[:, :width], ((1,), (1,)))
        low_back = dot(chosen[:, width:], block[:, width:], ((1,), (1,)))
        both[0, s * rank : (s + 1) * rank, :] = low_in.astype(BF)
        both[1, s * rank : (s + 1) * rank, :] = low_back.astype(BF)
    mine[...] = both[core]
    his[...] = both[1 - core]


def low(tables, firsts, blocks, rank, rows, size, owned):
    wide = blocks[0].shape[1]
    total = sum(table.shape[0] for table in tables)
    return pl.pallas_call(
        functools.partial(low_kernel, rank, rows, size, owned, firsts),
        in_specs=anywhere(len(tables) + len(blocks)),
        out_specs=vmem(2) + smem(),
        out_shape=[
            shape((2 * len(blocks) * rank, rows)),
            shape((2 * len(blocks) * rank, rows)),
            shape((2 * len(blocks),), jnp.int32),
        ],
        scratch_shapes=[
            pltpu.VMEM((total, wide), BF),
            pltpu.VMEM((len(blocks),) + blocks[0].shape, BF),
            pltpu.VMEM((2, 2 * len(blocks) * rank, rows), BF),
            pltpu.SemaphoreType.DMA((len(tables) + len(blocks),)),
        ],
        compiler_params=LARGE,
    )(*tables, *blocks)


def added(refs):
    total = refs[0][...].astype(F32)
    for ref in refs[1:]:
        total = total + ref[...].astype(F32)
    return total


def grad_kernel(rank, rows, parts, owned, names, *refs):
    lows, refs = refs[:parts], refs[parts:]
    groups = lows[0].shape[0] // (2 * rank)
    core = lax.rem(lax.axis_index("tensor"), 2)
    blocks, refs = refs[:groups], refs[groups:]
    *outs, sums, lows_here, here, half, sems, out_sems = refs
    width = sums.shape[2] - 128
    row = lax.axis_index("dp")
    span, size = owned * groups, len(outs) - 1
    copies = fetch(
        [*lows, *[ref.at[: 2 * rows, :] for ref in blocks]],
        [*[lows_here.at[d] for d in range(parts)], *[here.at[d] for d in range(groups)]],
        sems,
    )
    sums[...] = jnp.zeros_like(sums)
    for copy in copies[:parts]:
        copy.wait()
    for s in range(2 * groups):
        if s % 2 == 0:
            copies[parts + s // 2].wait()
        block = here[s // 2, (s % 2) * rows : (s % 2 + 1) * rows, :]
        low_in = lows_here[core, s * rank : (s + 1) * rank, :]
        low_back = lows_here[1 - core, s * rank : (s + 1) * rank, :]
        name = names[s]
        place = lax.rem(name // span - row + size, size) * owned + lax.rem(name, owned)
        sums[place, :, :width] += dot(low_back, block[:, :width], ((1,), (0,)))
        sums[place, :, width:] += dot(low_in, block[:, width:], ((1,), (0,)))
    stores = []
    far = size // 2
    order = [3, 5, far, 2, 6, 1, 7, 0]
    for d in order:
        for j in range(2):
            half[d, j * rank : (j + 1) * rank, :] = (adapter_scale * sums[2 * d + j]).astype(BF)
        if d == far:
            ends = [(half.at[d, :rank], outs[far]), (half.at[d, rank:], outs[-1])]
        else:
            ends = [(half.at[d], outs[d])]
        for source, out in ends:
            stores.append(pltpu.make_async_copy(source, out, out_sems.at[len(stores)]))
            stores[-1].start()
    for store in stores:
        store.wait()


def grad(names, lows, blocks, rank, rows, targets, owned):
    wide = blocks[0].shape[1]
    return pl.pallas_call(
        functools.partial(grad_kernel, rank, rows, len(lows), owned),
        in_specs=smem() + anywhere(len(lows) + len(blocks)),
        out_specs=anywhere(targets + 1),
        out_shape=[
            shape((rank if d in (targets // 2, targets) else 2 * rank, wide))
            for d in range(targets + 1)
        ],
        scratch_shapes=[
            pltpu.VMEM((2 * targets, rank, wide), F32),
            pltpu.VMEM((len(lows),) + lows[0].shape, BF),
            pltpu.VMEM((len(blocks), 2 * rows, wide), BF),
            pltpu.VMEM((targets, 2 * rank, wide), BF),
            pltpu.SemaphoreType.DMA((len(lows) + len(blocks),)),
            pltpu.SemaphoreType.DMA((targets + 1,)),
        ],
        compiler_params=LARGE,
    )(names, *lows, *blocks)


def adam_update(weights, moment, second, gradient):
    moment_new = beta_one * moment + (1.0 - beta_one) * gradient
    second_new = beta_two * second + (1.0 - beta_two) * gradient * gradient
    unbiased_m = moment_new / (1.0 - beta_one**STEP_NUM)
    unbiased_v = second_new / (1.0 - beta_two**STEP_NUM)
    weights_new = weights - step_rate * unbiased_m / (jnp.sqrt(unbiased_v) + adam_eps)
    return (weights_new, moment_new, second_new)


def adam_kernel(parts, *refs):
    grads, refs = refs[:parts], refs[parts:]
    states, outs, refs = refs[:6], refs[6:13], refs[13:]
    here, olds, news, fresh, sems, out_sems = refs[0], refs[1:7], refs[7:13], *refs[13:]
    copies = fetch([*states, *grads], [*olds, *[here.at[d] for d in range(parts)]], sems)
    width = olds[0].shape[1]
    for copy in copies:
        copy.wait()
    total = added([here.at[d] for d in range(parts)])
    for first, cols in ((0, slice(0, width)), (3, slice(width, None))):
        values = adam_update(*[ref[...] for ref in olds[first : first + 3]], total[:, cols])
        for ref, value in zip(news[first : first + 3], values):
            ref[...] = value
        fresh[:, cols] = values[0].astype(BF)
    for store in fetch([*news, fresh], outs, out_sems):
        store.wait()


def adam(grads, state_a, state_b):
    rows, width = state_a[0].shape
    width_b = state_b[0].shape[1]
    wide = width + width_b
    states = [pltpu.VMEM((rows, width), F32)] * 3 + [pltpu.VMEM((rows, width_b), F32)] * 3
    return pl.pallas_call(
        functools.partial(adam_kernel, len(grads)),
        in_specs=anywhere(len(grads) + 6),
        out_specs=anywhere(7),
        out_shape=[shape((rows, width), F32)] * 3
        + [shape((rows, width_b), F32)] * 3
        + [shape((rows, wide))],
        scratch_shapes=[pltpu.VMEM((len(grads), rows, wide), BF)]
        + states
        + states
        + [
            pltpu.VMEM((rows, wide), BF),
            pltpu.SemaphoreType.DMA((len(grads) + 6,)),
            pltpu.SemaphoreType.DMA((7,)),
        ],
        compiler_params=LARGE,
    )(*grads, *state_a, *state_b)


def pick_kernel(rank, index, *refs):
    *refs, out = refs
    for i in range(2):
        device, slot = index[i] // 2, index[i] % 2
        for d, ref in enumerate(refs):

            @pl.when(device == d)
            def _():
                out[i * rank : (i + 1) * rank, :] = block_of(ref, slot, rank)[...]


def pick(index, arrays, rank):
    return pl.pallas_call(
        functools.partial(pick_kernel, rank),
        in_specs=smem(1) + vmem(len(arrays)),
        out_specs=vmem()[0],
        out_shape=shape(arrays[0].shape),
        compiler_params=SMALL,
    )(index, *arrays)


def decode_in_kernel(rank, firsts, parts, slots, before, *refs):
    xs, refs = refs[:parts], refs[parts:]
    *refs, out = refs
    width = xs[0].shape[1]
    count = xs[0].shape[0]
    for i, x in enumerate(xs):
        here = slots[:, i * count : (i + 1) * count]
        total = before[:, i * count : (i + 1) * count]
        for first, ref in zip(firsts, refs):
            both = dot(ref[:, :width], x[...], ((1,), (1,)))
            for j in range(ref.shape[0] // rank):
                total += jnp.where(here == first + j, both[j * rank : (j + 1) * rank], 0.0)
        out[:, i * count : (i + 1) * count] = total


def decode_in(slots, before, xs, fresh, firsts, rank):
    return pl.pallas_call(
        functools.partial(decode_in_kernel, rank, firsts, len(xs)),
        in_specs=vmem(2 + len(xs) + len(fresh)),
        out_specs=vmem()[0],
        out_shape=shape((rank, slots.shape[1]), F32),
        compiler_params=SMALL,
    )(slots, before, *xs, *fresh)


def decode_out_kernel(rank, parts, firsts, slots, *refs):
    frozen, refs = refs[:2], refs[2:]
    lows, fresh, out = refs[:parts], refs[parts:-1], refs[-1]
    width_b = out.shape[1]
    total = added(lows).astype(BF).astype(F32)
    result = jnp.concatenate([ref[...] for ref in frozen], axis=0)
    for first, ref in zip(firsts, fresh):
        wide = ref.shape[1]
        both = jnp.concatenate(
            [jnp.where(slots[...] == first + j, total, 0.0) for j in range(ref.shape[0] // rank)],
            axis=0,
        )
        part = dot(both.T.astype(BF), ref[:, wide - width_b :], ((1,), (0,)))
        result += adapter_scale * part
    out[...] = result.astype(BF)


def decode_out(slots, frozen, lows, fresh, firsts, rank):
    return pl.pallas_call(
        functools.partial(decode_out_kernel, rank, len(lows), firsts),
        in_specs=vmem(1 + len(frozen) + len(lows) + len(fresh)),
        out_specs=vmem()[0],
        out_shape=shape((slots.shape[1], frozen[0].shape[1])),
        compiler_params=SMALL,
    )(slots, *frozen, *lows, *fresh)


def add(x, *more):
    total = x.astype(F32)
    for y in more:
        total = total + y.astype(F32)
    return total.astype(x.dtype)


def other_core(x):
    size = lax.axis_size("tensor")
    return lax.ppermute(x, "tensor", [(i, i ^ 1) for i in range(size)])


def chips(x):
    size = lax.axis_size("tensor")
    return [
        lax.ppermute(x, "tensor", [(i, (i + 2 * d) % size) for i in range(size)])
        for d in range(1, size // 2)
    ]


def tensor_parts(x):
    x = add(x, other_core(x))
    return [x, *chips(x)]


def local(
    learn_x,
    learn_dy,
    block_tenant,
    block_count,
    adapter_a,
    adapter_b,
    moment_a,
    moment_b,
    second_a,
    second_b,
    tenant_group,
    decode_inputs,
    dec_weight,
    request_adapter,
):
    groups = lax.axis_size("group")
    rows_dp = lax.axis_size("dp")
    group = lax.axis_index("group")
    row = lax.axis_index("dp")
    owned, rank, width = adapter_a.shape
    width_b = adapter_b.shape[2]
    span = groups * owned
    barrier = lax.optimization_barrier

    def flat(x):
        return x.reshape(owned * rank, x.shape[2])

    blocks = block_tenant.shape[0]
    rows = learn_x.shape[0] // blocks
    packed = begin(block_tenant, block_count, learn_x, learn_dy, groups)
    packed, state = barrier((packed, (adapter_a, adapter_b)))
    order = sorted(range(1, groups), key=lambda d: min(d, groups - d))
    moved = {d: shift(packed[d], "group", d) for d in order}
    arrived = [packed[0]] + [moved[d] for d in range(1, groups)]
    own = jnp.concatenate([flat(x).astype(BF) for x in state], axis=1)
    tables, firsts = ring(own, rows_dp, owned)
    requests = decode_inputs[0]
    steps = requests.shape[1]
    tensor = lax.axis_index("tensor").reshape(1)
    tables, requests = barrier((tables, requests))
    early = frozen(tensor, requests, dec_weight, 0, 2, width, WHOLE)
    arrived, tables, early = barrier((arrived, tables, early))

    mine, his, names = low(tables, firsts, arrived, rank, rows, rows_dp, owned)
    mine = add(mine, other_core(his))
    mine = add(mine, *chips(mine))
    lows = [mine, other_core(mine)]
    sums = grad(names, lows, arrived, rank, rows, rows_dp, owned)
    pieces = [sums[0], *two_stage_reduce(sums, rows_dp)]
    *new, fresh = adam(
        pieces,
        [flat(x) for x in (adapter_a, moment_a, second_a)],
        [flat(x) for x in (adapter_b, moment_b, second_b)],
    )

    tenant_ids = jnp.arange(tenant_group.shape[0], dtype=jnp.int32)
    served = (tenant_group == group).astype(jnp.int32)
    by_row = served.reshape(rows_dp, span)
    slot_of = jnp.cumsum(by_row, axis=1) - by_row
    mine = lax.dynamic_slice_in_dim(by_row, row, 1, 0)[0]
    mine_slot = lax.dynamic_slice_in_dim(slot_of, row, 1, 0)[0]
    position = jnp.arange(span, dtype=jnp.int32)
    relative = ((group - position // owned) % groups) * owned + position % owned
    wanted = jnp.sum(
        jnp.where(
            (mine[None, :] == 1)
            & (mine_slot[None, :] == jnp.arange(owned, dtype=jnp.int32)[:, None]),
            relative[None, :],
            0,
        ),
        axis=1,
        dtype=jnp.int32,
    )
    slot_here = ((row - tenant_ids // span) % rows_dp) * owned + slot_of.reshape(-1)
    slot_here = jnp.where(served == 1, slot_here, -1)
    request_slot = jnp.sum(
        jnp.where(request_adapter[0][:, None] == tenant_ids[None, :], slot_here[None, :], 0),
        axis=1,
        dtype=jnp.int32,
    )
    count = requests.shape[0] * steps
    slots = jnp.broadcast_to(request_slot[:, None], (requests.shape[0], steps)).reshape(1, count)
    *new, fresh = adam(
        pieces,
        [flat(x) for x in (adapter_a, moment_a, second_a)],
        [flat(x) for x in (adapter_b, moment_b, second_b)],
    )
    in_row = spread(fresh, "group")
    fresh, wanted, slots, requests = barrier((fresh, wanted, slots, requests))
    late = frozen(tensor, requests, dec_weight, 1, 2, width, MIDDLE)
    in_row, wanted, slots, late = barrier((in_row, wanted, slots, late))
    served_fresh, firsts = two_stage(pick(wanted, in_row, rank), rows_dp, owned)

    near, xs = 5, [early[1], late[1]]
    dec_part = jnp.zeros((rank, count), F32)
    dec_part = decode_in(slots, dec_part, xs, served_fresh[:near], firsts[:near], rank)
    dec_part = decode_in(slots, dec_part, xs, served_fresh[near:], firsts[near:], rank)
    decoded = decode_out(
        slots, [early[0], late[0]], tensor_parts(dec_part), served_fresh, firsts, rank
    )
    new_a = [x.reshape(adapter_a.shape) for x in new[:3]]
    new_b = [x.reshape(adapter_b.shape) for x in new[3:]]
    return (
        new_a[0],
        new_b[0],
        new_a[1],
        new_b[1],
        new_a[2],
        new_b[2],
        decoded.reshape((1,) + requests.shape[:2] + (width_b,)),
    )


def solution(mesh):
    state = P(("dp", "group"), None, "tensor")
    return jax.shard_map(
        local,
        mesh=mesh,
        in_specs=(
            P(("dp", "group"), "tensor"),
            P(("dp", "group"), "tensor"),
            P(("dp", "group")),
            P(("dp", "group")),
            state,
            state,
            state,
            state,
            state,
            state,
            P(),
            P("group", "dp", None, None),
            P(None, "tensor"),
            P("group", "dp"),
        ),
        out_specs=(
            state,
            state,
            state,
            state,
            state,
            state,
            P("group", "dp", None, "tensor"),
        ),
        check_vma=False,
    )
```
